32 devices in a mesh: runs: 2 (over x), sec: 16 (over z, y, core).
Axes of the slice: x: 2, y: 2, z: 4, core: 2. Of those that a mesh axis runs over, the one named last changes fastest.
Arguments:
- edge_rows: bfloat16 [4096, 1024], P(('runs', 'sec')), parts along dimension 0, may hold values from -46 to 46
- corner: bfloat16 [32768, 1024], P(('runs', 'sec')), parts along dimension 0, may hold values from -1 to 2.2
- joining: int32 [32, 16], P('runs'), parts along dimension 0, may hold values from 0 to 15, as said below
- charge_left: int32 [4096], P(('runs', 'sec')), parts along dimension 0, may hold values from 0 to 15
- charge_right: int32 [4096], P(('runs', 'sec')), parts along dimension 0, may hold values from 0 to 15
Outputs:
- isometry: float32 [4096, 1024], P(('runs', 'sec')), parts along dimension 0
The draws below stay inside these ranges and needn't reach their ends.
There are 2 independent parts, one for each index of `runs`. The reference program is written for one: setup_inputs(seed, part) draws one part's arguments, and reference() takes and returns one part's arrays. A program takes and returns all parts, laid end to end along the dimension named above; each array names one. Nothing has to cross between parts.
Inputs may be any that keep to these rules, and one draw needn't show every extreme that they name: joining[charge_left[e], charge_right[e]] names the block that row e needs; each row of joining names every block once; among the 128 rows of one device at most 16 need the same block, and one block, drawn per copy, receives exactly 16 rows from every device.
All inputs are finite; a program needn't handle non-finite values.
Results may differ from the reference program's by a relative error of at most 0.0003.
Values may be sent and summed in bfloat16 or wider, within the bound.
No kernel may reach another device: no remote copies, remote signals or barrier semaphores. Data moves between devices by JAX's collectives and lax.ppermute only.
A program may use at most 128 MiB of HBM per device.

```python
import math
import jax
import jax.numpy as jnp
from jax import lax

W = 1024
ROWS = 128
BLOCKS = 16
CAP = 16
EDGES = 2048


def route_plan(key):
    perm = jax.random.permutation(jax.random.fold_in(key, 11), BLOCKS).astype(jnp.int32)
    hot_block = jax.random.randint(jax.random.fold_in(key, 12), (), 0, BLOCKS)
    popular = jax.random.randint(jax.random.fold_in(key, 13), (BLOCKS,), 0, 1 << 14)
    slots = BLOCKS * CAP
    slot_block = jnp.arange(slots, dtype=jnp.int32) // CAP

    def one_source(source):
        source_key = jax.random.fold_in(jax.random.fold_in(key, 14), source)
        noise = jax.random.randint(source_key, (slots,), 0, 1 << 14)
        score = (noise + popular[slot_block]) * 4096 + jnp.arange(slots, dtype=jnp.int32)
        score = score + jnp.where(slot_block == hot_block, 1 << 29, 0)
        chosen = lax.top_k(score, ROWS)[1]
        chosen = jax.random.permutation(jax.random.fold_in(source_key, 1), chosen)
        return slot_block[chosen]
    target = jax.vmap(one_source)(jnp.arange(BLOCKS, dtype=jnp.int32)).reshape(-1)
    left = jax.random.randint(jax.random.fold_in(key, 15), (EDGES,), 0, BLOCKS)
    inverse = jnp.argsort(perm).astype(jnp.int32)
    right = (inverse[target] - left) % BLOCKS
    grid_a = jnp.arange(BLOCKS, dtype=jnp.int32)[:, None]
    grid_b = jnp.arange(BLOCKS, dtype=jnp.int32)[None, :]
    table = perm[(grid_a + grid_b) % BLOCKS]
    return (table, left, right)


def draw_joining(key, part):
    return route_plan(key)[0]


def draw_charge_left(key, part):
    return route_plan(key)[1]


def draw_charge_right(key, part):
    return route_plan(key)[2]


def draw_edge_rows(key, part):
    position = jnp.arange(EDGES, dtype=jnp.float32)[:, None] / EDGES
    rising = jnp.exp(math.log(3.0) * position)
    row_scale = jnp.exp(jax.random.uniform(jax.random.fold_in(key, 2), (EDGES, 1), minval=math.log(0.3), maxval=math.log(3.0)))
    base = jnp.clip(jax.random.normal(jax.random.fold_in(key, 1), (EDGES, W)), -5.0, 5.0)
    return (base * row_scale * rising).astype(jnp.bfloat16)


def draw_corner(key, part):
    row_index = jnp.arange(BLOCKS * W, dtype=jnp.int32)[:, None] % W
    col_index = jnp.arange(W, dtype=jnp.int32)[None, :]
    on_diag = row_index == col_index
    diag_value = jnp.exp(jax.random.uniform(jax.random.fold_in(key, 1), (BLOCKS * W, W), minval=0.0, maxval=math.log(2.0)))
    spread = jnp.clip(jax.random.normal(jax.random.fold_in(key, 2), (BLOCKS * W, W)), -5.0, 5.0)
    off_value = spread * (0.5 / math.sqrt(W))
    return jnp.where(on_diag, diag_value, off_value).astype(jnp.bfloat16)


def setup_inputs(seed: int = 0, part: int = 0) -> dict:
    keys = jax.random.split(jax.random.key(seed), 6)
    part_keys = jax.random.split(jax.random.fold_in(keys[5], part), 6)
    return {
        "edge_rows": draw_edge_rows(jax.random.fold_in(jax.random.fold_in(keys[5], part), 71), part),
        "corner": draw_corner(jax.random.fold_in(jax.random.fold_in(keys[5], part), 71), part),
        "joining": draw_joining(jax.random.fold_in(jax.random.fold_in(keys[5], part), 71), part),
        "charge_left": draw_charge_left(jax.random.fold_in(jax.random.fold_in(keys[5], part), 71), part),
        "charge_right": draw_charge_right(jax.random.fold_in(jax.random.fold_in(keys[5], part), 71), part),
    }


def reference(edge_rows, corner, joining, charge_left, charge_right):
    target = joining[charge_left, charge_right]
    count = BLOCKS * CAP

    def one_block(carry, block):
        picked = jnp.nonzero(target == block, size=count, fill_value=EDGES)[0]
        taken = jnp.take(edge_rows, picked, axis=0, mode='fill', fill_value=0).astype(jnp.float32)
        weight = lax.dynamic_slice_in_dim(corner, (block * W).astype(jnp.int32), W, 0).astype(jnp.float32)
        image = jnp.dot(taken, weight, precision=lax.Precision.HIGHEST)
        carry = carry.at[picked].set(image, mode='drop')
        return (carry, None)
    images, _ = lax.scan(one_block, jnp.zeros((EDGES, W), jnp.float32), jnp.arange(BLOCKS, dtype=jnp.int32))
    gram = lax.dot_general(images, images, (((0,), (0,)), ((), ())), precision=lax.Precision.HIGHEST)
    lower = jnp.linalg.cholesky(gram)
    solved = lax.linalg.triangular_solve(lower, images, left_side=False, lower=True, transpose_a=True)
    return solved * math.sqrt(EDGES)
```

```python
import functools
import math

import jax
import jax.numpy as jnp
from jax import lax
from jax.experimental import pallas as pl
from jax.experimental.pallas import tpu as pltpu
from jax.sharding import PartitionSpec as P

SIDE = 128
HIGHEST = lax.Precision.HIGHEST


def column_offsets(count):
    offsets = [0]
    for j in range(count):
        offsets.append(offsets[-1] + (count - j) * SIDE)
    return offsets


def dot_nt(a, b):
    return lax.dot_general(
        a, b, (((1,), (1,)), ((), ())), precision=HIGHEST, preferred_element_type=jnp.float32
    )


def dot_tn(a, b):
    return lax.dot_general(
        a, b, (((0,), (0,)), ((), ())), precision=HIGHEST, preferred_element_type=jnp.float32
    )


def images_kernel(arrived_ref, corner_ref, images_ref, gram_ref):
    width = corner_ref.shape[1]
    count = width // SIDE
    offsets = column_offsets(count)
    images = jnp.dot(arrived_ref[...], corner_ref[...], preferred_element_type=jnp.float32)
    images_ref[...] = images
    for j in range(0, count, 2):
        part = dot_tn(images[:, j * SIDE :], images[:, j * SIDE : (j + 2) * SIDE])
        gram_ref[offsets[j] : offsets[j + 1], :] = part[:, :SIDE]
        gram_ref[offsets[j + 1] : offsets[j + 2], :] = part[SIDE:, SIDE:]


def invert_factor(block):
    size = block.shape[0]
    lane = lax.broadcasted_iota(jnp.int32, (8, size), 1)
    sub = lax.broadcasted_iota(jnp.int32, (8, size), 0)

    def spread(x):
        return jnp.broadcast_to(x, (8, size))

    groups = size // 8
    for m in range(groups):
        g = 8 * m
        inside = (lane >= g) & (lane < g + 8)
        pivots = block[g : g + 8, :]
        columns = [spread(pivots[:, g + j : g + j + 1]) for j in range(8)]
        pivots = jnp.where(inside, (lane - g == sub).astype(jnp.float32), pivots)
        rows, below = {}, {}
        for r in range(m + 1, groups):
            x = block[8 * r : 8 * r + 8, :]
            below[r] = [spread(x[:, g + j : g + j + 1]) for j in range(8)]
            rows[r] = jnp.where(inside, 0.0, x)
        diagonal = columns[0]
        for j in range(8):
            inverse = 1.0 / spread(columns[j][j : j + 1, :])
            pivot_row = spread(pivots[j : j + 1, :])
            if j:
                diagonal = jnp.where(sub == j, columns[j], diagonal)
            weight = jnp.where(sub > j, columns[j], 0.0) * inverse
            pivots = pivots - weight * pivot_row
            heads = {k: spread(columns[k][j : j + 1, :]) for k in range(j + 1, 8)}
            for k in range(j + 1, 8):
                columns[k] = columns[k] - weight * heads[k]
            for r in range(m + 1, groups):
                weight_r = below[r][j] * inverse
                rows[r] = rows[r] - weight_r * pivot_row
                for k in range(j + 1, 8):
                    below[r][k] = below[r][k] - weight_r * heads[k]
        block[g : g + 8, :] = pivots * lax.rsqrt(diagonal)
        for r in range(m + 1, groups):
            block[8 * r : 8 * r + 8, :] = rows[r]


def cholesky_kernel(count, gram_ref, lower_ref, block):
    offsets = column_offsets(count)
    row = lax.broadcasted_iota(jnp.int32, (SIDE, SIDE), 0)
    col = lax.broadcasted_iota(jnp.int32, (SIDE, SIDE), 1)
    lower_ref[...] = gram_ref[...]

    def update(k):
        if k == count - 1:
            return
        top, bottom = offsets[k] + SIDE, offsets[k + 1]
        panel = dot_nt(lower_ref[top:bottom, :], lower_ref[offsets[k] : top, :])
        lower_ref[top:bottom, :] = panel
        for j in range(k + 1, count):
            first = (j - k - 1) * SIDE
            lower_ref[offsets[j] : offsets[j + 1], :] -= dot_nt(
                panel[first:], panel[first : first + SIDE]
            )

    def step(k, carry):
        start = pl.multiple_of((k * count - (k * (k - 1)) // 2) * SIDE, SIDE)
        block[...] = lower_ref[pl.ds(start, SIDE), :]
        invert_factor(block)
        lower_ref[pl.ds(start, SIDE), :] = jnp.where(col <= row, block[...], 0.0)
        for kk in range(count):
            pl.when(k == kk)(functools.partial(update, kk))
        return carry

    lax.fori_loop(0, count, step, 0)


def solve_kernel(count, factor, home_ref, lower_ref, out_ref, rest):
    offsets = column_offsets(count)
    rest[...] = home_ref[...]
    for k in range(count):
        here = slice(k * SIDE, (k + 1) * SIDE)
        top = offsets[k] + SIDE
        solved = dot_nt(rest[:, here], lower_ref[offsets[k] : top, :])
        out_ref[:, here] = solved * factor
        if k < count - 1:
            rest[:, (k + 1) * SIDE :] -= dot_nt(solved, lower_ref[top : offsets[k + 1], :])


def kernel_call(kernel, out_shape, scratch=()):
    return pl.pallas_call(
        kernel,
        out_shape=out_shape,
        scratch_shapes=list(scratch),
        compiler_params=pltpu.CompilerParams(vmem_limit_bytes=40 << 20),
    )


def swap(x, bit):
    return lax.ppermute(x, "sec", [(i, i ^ bit) for i in range(lax.axis_size("sec"))])


def halve(x, bit):
    upper = (lax.axis_index("sec") // bit) % 2
    half = x.shape[0] // 2
    sent = lax.dynamic_slice_in_dim(x, (1 - upper) * half, half, 0)
    kept = lax.dynamic_slice_in_dim(x, upper * half, half, 0)
    return kept + swap(sent, bit)


def double(x, bit):
    upper = (lax.axis_index("sec") // bit) % 2 == 1
    other = swap(x, bit)
    return jnp.where(
        upper, jnp.concatenate([other, x], axis=0), jnp.concatenate([x, other], axis=0)
    )


def reduce_gram(packed):
    bits = [1 << b for b in range(1, lax.axis_size("sec").bit_length() - 1)]
    cut = len(bits) // 2
    orders = [bits, bits[cut:] + bits[:cut]]
    mine = halve(packed, 1)
    streams = []
    for order, part in zip(orders, jnp.split(mine, 2, axis=0)):
        for bit in order:
            part = halve(part, bit)
        streams.append(part)
    whole = []
    for order, part in zip(orders, streams):
        for bit in reversed(order):
            part = double(part, bit)
        whole.append(part)
    return double(jnp.concatenate(whole, axis=0), 1)


def per_device(edge_rows, corner, joining, charge_left, charge_right):
    row_count, feature_len = edge_rows.shape
    owners = lax.axis_size("sec")
    capacity = 2 * row_count // owners
    slots = owners * capacity
    factor = math.sqrt(row_count * owners)
    count = feature_len // SIDE
    packed_rows = column_offsets(count)[-1]
    f32 = jnp.float32
    target = joining[charge_left, charge_right]
    labels = jnp.arange(owners, dtype=jnp.int32)
    onehot = (target[:, None] == labels[None, :]).astype(jnp.int32)
    before = jnp.cumsum(onehot, axis=0) - onehot
    order_in = jnp.sum(before * onehot, axis=1)
    slot_index = target * capacity + order_in
    packed = jnp.zeros((slots, feature_len), edge_rows.dtype).at[slot_index].set(edge_rows)
    arrived = lax.all_to_all(
        packed.reshape(owners, capacity, feature_len), "sec", split_axis=0, concat_axis=0, tiled=True
    )
    product, gram = kernel_call(
        images_kernel,
        (
            jax.ShapeDtypeStruct((slots, feature_len), f32),
            jax.ShapeDtypeStruct((packed_rows, SIDE), f32),
        ),
    )(arrived.reshape(slots, feature_len), corner)
    returned = lax.all_to_all(
        product.reshape(owners, capacity, feature_len), "sec", split_axis=0, concat_axis=0, tiled=True
    )
    total = reduce_gram(gram)
    lower = kernel_call(
        functools.partial(cholesky_kernel, count),
        jax.ShapeDtypeStruct((packed_rows, SIDE), f32),
        [pltpu.VMEM((SIDE, SIDE), f32)],
    )(total)
    home_rows = returned.reshape(slots, feature_len)[slot_index]
    return kernel_call(
        functools.partial(solve_kernel, count, factor),
        jax.ShapeDtypeStruct((row_count, feature_len), f32),
        [pltpu.VMEM((row_count, feature_len), f32)],
    )(home_rows, lower)


def solution(mesh):
    placed = (
        P(("runs", "sec"), None),
        P(("runs", "sec"), None),
        P("runs", None),
        P(("runs", "sec")),
        P(("runs", "sec")),
    )
    return jax.shard_map(
        per_device, mesh=mesh, in_specs=placed, out_specs=P(("runs", "sec"), None), check_vma=False
    )
```

```python
import functools
import math

import jax
import jax.numpy as jnp
from jax import lax
from jax.experimental import pallas as pl
from jax.experimental.pallas import tpu as pltpu
from jax.sharding import PartitionSpec as P

SIDE = 128


def column_offsets(count):
    offsets = [0]
    for j in range(count):
        offsets.append(offsets[-1] + (count - j) * SIDE)
    return offsets


def split(x):
    high = x.astype(jnp.bfloat16)
    return high, (x - high.astype(jnp.float32)).astype(jnp.bfloat16)


def left(x, axis):
    high, low = split(x)
    return jnp.concatenate([high, high, low], axis=axis)


def right(x, axis):
    high, low = split(x)
    return jnp.concatenate([high, low, high], axis=axis)


def dot_nt(a, b):
    return lax.dot_general(a, b, (((1,), (1,)), ((), ())), preferred_element_type=jnp.float32)


def dot_tn(a, b):
    return lax.dot_general(a, b, (((0,), (0,)), ((), ())), preferred_element_type=jnp.float32)


def iota(shape, axis):
    return lax.broadcasted_iota(jnp.int32, shape, axis)


def route_kernel(capacity, edge_ref, joining_ref, left_ref, right_ref, slot_ref, packed_ref):
    bf16 = jnp.bfloat16
    rows = edge_ref.shape[0]
    owners = joining_ref.shape[0]
    slots = packed_ref.shape[0]
    one = lambda hit: hit.astype(jnp.float32)
    label = iota((owners, rows), 0)
    is_left = one(label == left_ref[...]).astype(bf16)
    options = dot_tn(joining_ref[...].astype(jnp.float32).astype(bf16), is_left)
    target = jnp.sum(jnp.where(label == right_ref[...], options, 0.0), axis=0, keepdims=True)
    is_target = label.astype(jnp.float32) == target
    earlier = one(iota((rows, rows), 0) < iota((rows, rows), 1)).astype(bf16)
    before = jnp.dot(one(is_target).astype(bf16), earlier, preferred_element_type=jnp.float32)
    order = jnp.sum(jnp.where(is_target, before, 0.0), axis=0, keepdims=True)
    slot = (target * capacity + order).astype(jnp.int32)
    slot_ref[...] = slot
    placed = one(iota((slots, rows), 0) == slot).astype(bf16)
    packed_ref[...] = jnp.dot(
        placed, edge_ref[...], preferred_element_type=jnp.float32
    ).astype(bf16)


def images_kernel(arrived_ref, corner_ref, images_ref, gram_ref):
    width = corner_ref.shape[1]
    count = width // SIDE
    offsets = column_offsets(count)
    images = jnp.dot(arrived_ref[...], corner_ref[...], preferred_element_type=jnp.float32)
    images_ref[...] = images
    first, second = left(images, 0), right(images, 0)
    for j in range(0, count, 2):
        part = dot_tn(first[:, j * SIDE :], second[:, j * SIDE : (j + 2) * SIDE])
        gram_ref[offsets[j] : offsets[j + 1], :] = part[:, :SIDE]
        gram_ref[offsets[j + 1] : offsets[j + 2], :] = part[SIDE:, SIDE:]


def eliminate(rows, start):
    shape = rows[0].shape
    lane, sub = iota(shape, 1), iota(shape, 0)
    rows = list(rows)
    groups = len(rows)

    def spread(x):
        return jnp.broadcast_to(x, shape)

    def columns_of(x, first):
        return [spread(x[:, first + j : first + j + 1]) for j in range(8)]

    pivots = columns_of(rows[0], start)
    for m in range(groups):
        g = start + 8 * m
        later = range(m + 1, groups)
        inside = (lane >= g) & (lane < g + 8)
        current = rows[m]
        ahead, ahead_below = [], []
        if later:
            ahead = columns_of(current, g + 8)
            ahead_below = columns_of(rows[m + 1], g + 8)
        below = {r: columns_of(rows[r], g) for r in later}
        current = jnp.where(inside, (lane - g == sub).astype(jnp.float32), current)
        for r in later:
            rows[r] = jnp.where(inside, 0.0, rows[r])
        diagonal = pivots[0]
        for j in range(8):
            inverse = 1.0 / spread(pivots[j][j : j + 1, :])
            pivot_row = spread(current[j : j + 1, :])
            heads = [spread(x[j : j + 1, :]) for x in pivots[j + 1 :]]
            ahead_heads = [spread(x[j : j + 1, :]) for x in ahead]
            if j:
                diagonal = jnp.where(sub == j, pivots[j], diagonal)
            if j < 7:
                weight = jnp.where(sub > j, pivots[j], 0.0) * inverse
                current = current - weight * pivot_row
                for k, head in enumerate(heads, j + 1):
                    pivots[k] = pivots[k] - weight * head
                ahead = [x - weight * head for x, head in zip(ahead, ahead_heads)]
            for r in later:
                weight = below[r][j] * inverse
                rows[r] = rows[r] - weight * pivot_row
                for k, head in enumerate(heads, j + 1):
                    below[r][k] = below[r][k] - weight * head
                if r == m + 1:
                    ahead_below = [x - weight * head for x, head in zip(ahead_below, ahead_heads)]
        rows[m] = current * lax.rsqrt(diagonal)
        pivots = ahead_below
    return rows


def invert_factor(block):
    size = block.shape[0]
    half = size // 2
    groups = range(0, half, 8)
    lane, row = iota((half, size), 1), iota((half, size), 0)
    upper = jnp.concatenate(eliminate([block[g : g + 8, :] for g in groups], 0), axis=0)
    inverse = jnp.where((lane < half) & (lane > row), 0.0, upper)
    lower = jnp.where(lane < half, 0.0, block[half:, :])
    lower = lower - dot_tn(left(upper[:, half:], 0), right(inverse, 0))
    lower = jnp.concatenate(eliminate([lower[g : g + 8, :] for g in groups], half), axis=0)
    return jnp.concatenate(
        [jnp.where(lane < half, inverse, 0.0), jnp.where(lane <= row + half, lower, 0.0)], axis=0
    )


def cholesky_kernel(count, gram_ref, lower_ref):
    offsets = column_offsets(count)
    lower_ref[...] = gram_ref[...]

    def update(k, first, second, columns):
        for j in columns[::2]:
            top = (j - k - 1) * SIDE
            part = dot_nt(first[top:], second[top : top + 2 * SIDE])
            lower_ref[offsets[j] : offsets[j + 1], :] -= part[:, :SIDE]
            if j + 1 in columns:
                lower_ref[offsets[j + 1] : offsets[j + 2], :] -= part[SIDE:, SIDE:]

    previous = None
    for k in range(count):
        top, bottom = offsets[k] + SIDE, offsets[k + 1]
        inverse = invert_factor(lower_ref[offsets[k] : top, :])
        if previous is not None:
            update(k - 1, *previous, range(k + 1, count))
        lower_ref[offsets[k] : top, :] = inverse
        if k + 1 < count:
            panel = dot_nt(left(lower_ref[top:bottom, :], 1), right(inverse, 1))
            lower_ref[top:bottom, :] = panel
            previous = left(panel, 1), right(panel, 1)
            update(k, *previous, range(k + 1, k + 2))


def solve_kernel(count, factor, returned_ref, slot_ref, lower_ref, out_ref, rest):
    offsets = column_offsets(count)
    slots, rows = returned_ref.shape[0], slot_ref.shape[1]
    placed = (iota((slots, rows), 0) == slot_ref[...]).astype(jnp.float32).astype(jnp.bfloat16)
    high, low = split(returned_ref[...])
    rest[...] = dot_tn(placed, high) + dot_tn(placed, low)
    for k in range(count):
        here = slice(k * SIDE, (k + 1) * SIDE)
        top = offsets[k] + SIDE
        solved = dot_nt(left(rest[:, here], 1), right(lower_ref[offsets[k] : top, :], 1))
        out_ref[:, here] = solved * factor
        if k < count - 1:
            rest[:, (k + 1) * SIDE :] -= dot_nt(
                left(solved, 1), right(lower_ref[top : offsets[k + 1], :], 1)
            )


def kernel_call(kernel, out_shape, scratch=(), work=0):
    return pl.pallas_call(
        kernel,
        out_shape=out_shape,
        scratch_shapes=list(scratch),
        cost_estimate=pl.CostEstimate(flops=2 * work, bytes_accessed=0, transcendentals=0),
        compiler_params=pltpu.CompilerParams(vmem_limit_bytes=16 << 20),
    )


def swap(x, bit):
    return lax.ppermute(x, "sec", [(i, i ^ bit) for i in range(lax.axis_size("sec"))])


def halve(x, bit):
    upper = (lax.axis_index("sec") // bit) % 2
    half = x.shape[0] // 2
    sent = lax.dynamic_slice_in_dim(x, (1 - upper) * half, half, 0)
    kept = lax.dynamic_slice_in_dim(x, upper * half, half, 0)
    return kept + swap(sent, bit)


def double(x, bit):
    upper = (lax.axis_index("sec") // bit) % 2 == 1
    other = swap(x, bit)
    return jnp.where(
        upper, jnp.concatenate([other, x], axis=0), jnp.concatenate([x, other], axis=0)
    )


def reduce_gram(packed):
    bits = [1 << b for b in range(1, lax.axis_size("sec").bit_length() - 1)]
    cut = len(bits) // 2
    orders = [bits, bits[cut:] + bits[:cut]]
    mine = halve(packed, 1)
    streams = []
    for order, part in zip(orders, jnp.split(mine, 2, axis=0)):
        for bit in order:
            part = halve(part, bit)
        streams.append(part)
    whole = []
    for order, part in zip(orders, streams):
        for bit in reversed(order):
            part = double(part, bit)
        whole.append(part)
    return double(jnp.concatenate(whole, axis=0), 1)


def per_device(edge_rows, corner, joining, charge_left, charge_right):
    row_count, feature_len = edge_rows.shape
    owners = lax.axis_size("sec")
    capacity = 2 * row_count // owners
    slots = owners * capacity
    factor = math.sqrt(row_count * owners)
    count = feature_len // SIDE
    packed_rows = column_offsets(count)[-1]
    f32 = jnp.float32
    slot, packed = kernel_call(
        functools.partial(route_kernel, capacity),
        (
            jax.ShapeDtypeStruct((1, row_count), jnp.int32),
            jax.ShapeDtypeStruct((slots, feature_len), edge_rows.dtype),
        ),
    )(edge_rows, joining, charge_left[None, :], charge_right[None, :])
    arrived = lax.all_to_all(
        packed.reshape(owners, capacity, feature_len), "sec", split_axis=0, concat_axis=0, tiled=True
    )
    product, gram = kernel_call(
        images_kernel,
        (
            jax.ShapeDtypeStruct((slots, feature_len), f32),
            jax.ShapeDtypeStruct((packed_rows, SIDE), f32),
        ),
    )(arrived.reshape(slots, feature_len), corner)
    total = reduce_gram(gram)
    product, total = lax.optimization_barrier((product, total))
    returned = lax.all_to_all(
        product.reshape(owners, capacity, feature_len), "sec", split_axis=0, concat_axis=0, tiled=True
    )
    lower = kernel_call(
        functools.partial(cholesky_kernel, count),
        jax.ShapeDtypeStruct((packed_rows, SIDE), f32),
        work=20 * packed_rows * feature_len * feature_len,
    )(total)
    returned, lower = lax.optimization_barrier((returned, lower))
    return kernel_call(
        functools.partial(solve_kernel, count, factor),
        jax.ShapeDtypeStruct((row_count, feature_len), f32),
        [pltpu.VMEM((row_count, feature_len), f32)],
    )(returned.reshape(slots, feature_len), slot, lower)


def solution(mesh):
    placed = (
        P(("runs", "sec"), None),
        P(("runs", "sec"), None),
        P("runs", None),
        P(("runs", "sec")),
        P(("runs", "sec")),
    )
    return jax.shard_map(
        per_device, mesh=mesh, in_specs=placed, out_specs=P(("runs", "sec"), None), check_vma=False
    )
```

```python
import functools
import math

import jax
import jax.numpy as jnp
from jax import lax
from jax.experimental import pallas as pl
from jax.experimental.pallas import tpu as pltpu
from jax.sharding import PartitionSpec as P

SIDE = 128


def column_offsets(count):
    offsets = [0]
    for j in range(count):
        offsets.append(offsets[-1] + (count - j) * SIDE)
    return offsets


def split(x):
    high = x.astype(jnp.bfloat16)
    return high, (x - high.astype(jnp.float32)).astype(jnp.bfloat16)


def left(x, axis):
    high, low = split(x)
    return jnp.concatenate([high, high, low], axis=axis)


def right(x, axis):
    high, low = split(x)
    return jnp.concatenate([high, low, high], axis=axis)


def dot_nt(a, b):
    return lax.dot_general(a, b, (((1,), (1,)), ((), ())), preferred_element_type=jnp.float32)


def dot_tn(a, b):
    return lax.dot_general(a, b, (((0,), (0,)), ((), ())), preferred_element_type=jnp.float32)


def dot_nn(a, b):
    return jnp.dot(a, b, preferred_element_type=jnp.float32)


def iota(shape, axis):
    return lax.broadcasted_iota(jnp.int32, shape, axis)


def route_kernel(
    capacity, edge_hbm, joining_hbm, left_hbm, right_hbm, slot_ref, packed_ref,
    edge_ref, joining_ref, left_ref, right_ref, done,
):
    bf16 = jnp.bfloat16
    pairs = [
        (joining_hbm, joining_ref),
        (left_hbm, left_ref),
        (right_hbm, right_ref),
        (edge_hbm, edge_ref),
    ]
    copies = [pltpu.make_async_copy(a, b, done.at[i]) for i, (a, b) in enumerate(pairs)]
    for copy in copies:
        copy.start()
    rows = edge_ref.shape[0]
    owners = joining_ref.shape[0]
    slots = packed_ref.shape[0]
    one = lambda hit: hit.astype(jnp.float32)
    label = iota((owners, rows), 0)
    for copy in copies[:3]:
        copy.wait()
    is_left = one(label == left_ref[...]).astype(bf16)
    options = dot_tn(joining_ref[...].astype(jnp.float32).astype(bf16), is_left)
    target = jnp.sum(jnp.where(label == right_ref[...], options, 0.0), axis=0, keepdims=True)
    is_target = label.astype(jnp.float32) == target
    earlier = one(iota((rows, rows), 0) < iota((rows, rows), 1)).astype(bf16)
    before = jnp.dot(one(is_target).astype(bf16), earlier, preferred_element_type=jnp.float32)
    order = jnp.sum(jnp.where(is_target, before, 0.0), axis=0, keepdims=True)
    slot = (target * capacity + order).astype(jnp.int32)
    slot_ref[...] = slot
    placed = one(iota((slots, rows), 0) == slot).astype(bf16)
    copies[3].wait()
    packed_ref[...] = jnp.dot(
        placed, edge_ref[...], preferred_element_type=jnp.float32
    ).astype(bf16)


def fetch_kernel(mine_hbm, other_hbm, mine_ref, other_ref, done):
    copies = [
        pltpu.make_async_copy(mine_hbm, mine_ref, done.at[0]),
        pltpu.make_async_copy(other_hbm, other_ref, done.at[1]),
    ]
    for copy in copies:
        copy.start()
    for copy in copies:
        copy.wait()


def shares(count):
    pairs = list(range(count // 2))
    outer = [p for p in pairs if p % 4 in (0, 3)]
    return outer, [p for p in pairs if p not in outer]


def share_rows(count):
    offsets = column_offsets(count)
    full = (offsets[-1] - count // 2 * SIDE) // 2
    return (full + 128) // 2, full // 2


def images_kernel(
    core_ref, arrived_ref, other_arrived_ref, corner_ref, other_corner_ref, images_ref, gram_ref
):
    width = corner_ref.shape[1]
    count = width // SIDE
    others = dot_nn(other_arrived_ref[...], other_corner_ref[...])
    images = dot_nn(arrived_ref[...], corner_ref[...])
    images_ref[...] = images
    images = jnp.concatenate([images, others], axis=0)
    first, second = left(images, 0), right(images, 0)
    row, col = iota((SIDE, SIDE), 0), iota((SIDE, SIDE), 1)

    def store(at, x):
        gram_ref[at : at + x.shape[0], :] = x

    def share(pairs):
        at = 0
        diagonals = []
        for p in pairs:
            start = 2 * p * SIDE
            part = dot_tn(first[:, start:], second[:, start : start + 2 * SIDE])
            upper, lower = part[:SIDE, :SIDE], part[SIDE : 2 * SIDE, SIDE:]
            store(at, jnp.where(row >= col, upper, lower))
            store(at + SIDE, part[SIDE : 2 * SIDE, :SIDE])
            diagonals.append(jnp.sum(jnp.where(row == col, lower, 0.0), axis=0, keepdims=True))
            at += 2 * SIDE
            rest = width - start - 2 * SIDE
            if rest:
                store(at, part[2 * SIDE :, :SIDE])
                store(at + rest, part[2 * SIDE :, SIDE:])
                at += 2 * rest
        store(at, jnp.zeros((gram_ref.shape[0] - at, SIDE), jnp.float32))
        for i, diagonal in enumerate(diagonals):
            store(at + i, diagonal)

    for core, pairs in enumerate(shares(count)):
        pl.when(core_ref[0] == core)(functools.partial(share, pairs))


def unpack_share(count, core, parts, lower_ref, diagonal_ref, done):
    offsets = column_offsets(count)
    cut = parts[0].shape[0]
    copies = []

    def copy(target, source, rows):
        for ref, low in ((parts[0], 0), (parts[1], cut)):
            begin, end = max(source, low), min(source + rows, low + ref.shape[0])
            if begin < end:
                copies.append(
                    pltpu.make_async_copy(
                        ref.at[begin - low : end - low],
                        lower_ref.at[target + begin - source : target + end - source],
                        done.at[core, len(copies)],
                    )
                )

    at = 0
    for p in shares(count)[core]:
        first, second = offsets[2 * p], offsets[2 * p + 1]
        rest = (count - 2 * p - 2) * SIDE
        copy(first, at, 2 * SIDE)
        if rest:
            copy(first + 2 * SIDE, at + 2 * SIDE, rest)
            copy(second + SIDE, at + 2 * SIDE + rest, rest)
        at += 2 * SIDE + 2 * rest
    copies.append(
        pltpu.make_async_copy(
            parts[1].at[at - cut : at - cut + 8], diagonal_ref.at[core], done.at[core, len(copies)]
        )
    )
    return copies


def part_diagonals(count, core, lower_ref, diagonal_ref, which):
    offsets = column_offsets(count)
    row, col = iota((SIDE, SIDE), 0), iota((SIDE, SIDE), 1)
    for i, p in list(enumerate(shares(count)[core]))[which]:
        first, second = offsets[2 * p], offsets[2 * p + 1]
        both = lower_ref[first : first + SIDE, :]
        turned = both.T
        diagonal = diagonal_ref[core, i : i + 1, :]
        lower_ref[first : first + SIDE, :] = jnp.where(row >= col, both, turned)
        lower_ref[second : second + SIDE, :] = jnp.where(
            row == col, diagonal, jnp.where(row < col, both, turned)
        )


def eliminate(rows, start, tick):
    shape = rows[0].shape
    lane, sub = iota(shape, 1), iota(shape, 0)
    rows = list(rows)
    groups = len(rows)

    def spread(x):
        return jnp.broadcast_to(x, shape)

    def columns_of(x, first):
        return [spread(x[:, first + j : first + j + 1]) for j in range(8)]

    pivots = columns_of(rows[0], start)
    for m in range(groups):
        g = start + 8 * m
        later = range(m + 1, groups)
        inside = (lane >= g) & (lane < g + 8)
        current = rows[m]
        ahead, ahead_below = [], []
        if later:
            ahead = columns_of(current, g + 8)
            ahead_below = columns_of(rows[m + 1], g + 8)
        below = {r: columns_of(rows[r], g) for r in later}
        current = jnp.where(inside, (lane - g == sub).astype(jnp.float32), current)
        for r in later:
            rows[r] = jnp.where(inside, 0.0, rows[r])
        diagonal = pivots[0]
        for j in range(8):
            inverse = 1.0 / spread(pivots[j][j : j + 1, :])
            pivot_row = spread(current[j : j + 1, :])
            heads = [spread(x[j : j + 1, :]) for x in pivots[j + 1 :]]
            ahead_heads = [spread(x[j : j + 1, :]) for x in ahead]
            if j:
                diagonal = jnp.where(sub == j, pivots[j], diagonal)
            if j < 7:
                weight = jnp.where(sub > j, pivots[j], 0.0) * inverse
                current = current - weight * pivot_row
                for k, head in enumerate(heads, j + 1):
                    pivots[k] = pivots[k] - weight * head
                ahead = [x - weight * head for x, head in zip(ahead, ahead_heads)]
            for r in later:
                weight = below[r][j] * inverse
                rows[r] = rows[r] - weight * pivot_row
                for k, head in enumerate(heads, j + 1):
                    below[r][k] = below[r][k] - weight * head
                if r == m + 1:
                    ahead_below = [x - weight * head for x, head in zip(ahead_below, ahead_heads)]
        rows[m] = current * lax.rsqrt(diagonal)
        pivots = ahead_below
        tick()
    return rows


def invert_factor(block, beside=()):
    size = block.shape[0]
    half = size // 2
    groups = range(0, half, 8)
    ticks = 2 * len(groups)
    pending = [list(beside[t * len(beside) // ticks : (t + 1) * len(beside) // ticks]) for t in range(ticks)]
    pending.reverse()

    def tick():
        for piece in pending.pop():
            piece()

    lane, row = iota((half, size), 1), iota((half, size), 0)
    upper = jnp.concatenate(eliminate([block[g : g + 8, :] for g in groups], 0, tick), axis=0)
    inverse = jnp.where((lane < half) & (lane > row), 0.0, upper)
    lower = jnp.where(lane < half, 0.0, block[half:, :])
    lower = lower - dot_tn(left(upper[:, half:], 0), right(inverse, 0))
    lower = jnp.concatenate(
        eliminate([lower[g : g + 8, :] for g in groups], half, tick), axis=0
    )
    return jnp.concatenate(
        [jnp.where(lane < half, inverse, 0.0), jnp.where(lane <= row + half, lower, 0.0)], axis=0
    )


def join_inverses(low, between, high):
    middle = dot_nn(left(high, 1), right(dot_nn(left(between, 1), right(low, 0)), 0))
    return jnp.concatenate(
        [
            jnp.concatenate([low, jnp.zeros((low.shape[0], high.shape[1]), jnp.float32)], axis=1),
            jnp.concatenate([-middle, high], axis=1),
        ],
        axis=0,
    )


def cholesky_kernel(
    count, core_ref, mine0, mine1, other0, other1, inverse_hbm, across_hbm, next_hbm, beyond_hbm, tail_hbm,
    lower_ref, diagonal_ref, inverse_ref, across_ref, next_ref, beyond_ref, done, out_done,
):
    offsets = column_offsets(count)
    half, three = count // 2, 3 * count // 4
    for core in (0, 1):

        @pl.when(core_ref[0] == core)
        def _(core=core):
            copies = unpack_share(count, core, (mine0, mine1), lower_ref, diagonal_ref, done)
            copies += unpack_share(count, 1 - core, (other0, other1), lower_ref, diagonal_ref, done)
            for copy in copies:
                copy.start()

    arrivals = [
        unpack_share(count, core, (mine0, mine1), lower_ref, diagonal_ref, done) for core in (0, 1)
    ]
    arrivals[0][0].wait()
    arrivals[0][-1].wait()
    part_diagonals(count, 0, lower_ref, diagonal_ref, slice(0, 1))

    def arrive():
        for copy in arrivals[0][1:-1] + arrivals[1]:
            copy.wait()
        part_diagonals(count, 0, lower_ref, diagonal_ref, slice(1, None))
        part_diagonals(count, 1, lower_ref, diagonal_ref, slice(None))

    def at(i, j):
        first = offsets[j] + (i - j) * SIDE
        return slice(first, first + SIDE)

    def blocks(rows, columns):
        return jnp.concatenate(
            [lower_ref[at(rows[0], j).start : at(rows[-1], j).stop, :] for j in columns], axis=1
        )

    inverses = {}
    outward = []

    def send(ref, hbm):
        outward.append(pltpu.make_async_copy(ref, hbm, out_done.at[len(outward)]))
        outward[-1].start()

    def pair(p):
        def run():
            inverses[p] = join_inverses(
                lower_ref[at(p, p), :], lower_ref[at(p + 1, p), :], lower_ref[at(p + 1, p + 1), :]
            )

        return run

    def join_half():
        inverse_ref[...] = right(
            join_inverses(inverses[0], blocks(range(2, 4), range(2)), inverses[2]), 1
        )
        send(inverse_ref, inverse_hbm)

    def across():
        across_ref[...] = right(blocks(range(half, count), range(half)), 1)
        send(across_ref, across_hbm)

    def beyond():
        next_ref[...] = right(inverses[half], 1)
        beyond_ref[...] = right(blocks(range(three, count), range(half, three)), 1)
        send(next_ref, next_hbm)
        send(beyond_ref, beyond_hbm)

    extra = {2: [pair(0)], 4: [pair(2), join_half, across], 6: [pair(half), beyond]}

    def rest_of(k, head):
        pieces, forms = [], {}
        if k + 2 >= count:
            return pieces
        rest = slice(at(k + 2, k).start, offsets[k + 1])

        def panel():
            below = dot_nt(left(lower_ref[rest, :], 1), right(lower_ref[at(k, k), :], 1))
            lower_ref[rest, :] = below
            forms["left"], forms["right"] = left(below, 1), right(below, 1)

        def next_column():
            lower_ref[at(k + 2, k + 1).start : offsets[k + 2], :] -= dot_nt(
                forms["left"], right(head, 1)
            )

        def product(j, i):
            def run():
                high = min(i + 2, count)
                rows = slice((i - k - 2) * SIDE, (high - k - 2) * SIDE)
                columns = slice((j - k - 2) * SIDE, (min(j + 2, count) - k - 2) * SIDE)
                part = dot_nt(forms["left"][rows], forms["right"][columns])
                lower_ref[at(i, j).start : at(high - 1, j).stop, :] -= part[:, :SIDE]
                if j + 1 < count:
                    skip = SIDE if i == j else 0
                    lower_ref[at(max(i, j + 1), j + 1).start : at(high - 1, j + 1).stop, :] -= part[
                        skip:, SIDE:
                    ]

            return run

        pieces += [panel, next_column]
        for j in range(k + 2, count, 2):
            for i in range(j, count, 2):
                pieces.append(product(j, i))
        return pieces

    beside = [lambda: None] * 2 + [arrive]
    for k in range(count - 1):
        inverse = invert_factor(lower_ref[at(k, k), :], beside + extra.get(k, []))
        lower_ref[at(k, k), :] = inverse
        head = dot_nt(left(lower_ref[at(k + 1, k), :], 1), right(inverse, 1))
        lower_ref[at(k + 1, k), :] = head
        lower_ref[at(k + 1, k + 1), :] -= dot_nt(left(head, 1), right(head, 1))
        beside = rest_of(k, head)
    send(lower_ref.at[offsets[count - 2] :], tail_hbm)
    for copy in outward:
        copy.wait()


def solve_kernel(
    count, factor, slot_ref, tail_hbm, returned_hbm, inverse_hbm, across_hbm, next_hbm, beyond_hbm, out_ref,
    tail_ref, returned_ref, inverse_ref, across_ref, next_ref, beyond_ref, done,
):
    half, three = count // 2 * SIDE, 3 * count // 4 * SIDE
    pairs = [
        (tail_hbm, tail_ref),
        (returned_hbm, returned_ref),
        (inverse_hbm, inverse_ref),
        (across_hbm, across_ref),
        (next_hbm, next_ref),
        (beyond_hbm, beyond_ref),
    ]
    copies = [pltpu.make_async_copy(a, b, done.at[i]) for i, (a, b) in enumerate(pairs)]
    for copy in copies:
        copy.start()
    slots, rows = returned_ref.shape[0], slot_ref.shape[1]
    width = returned_ref.shape[1]
    placed = (iota((slots, rows), 0) == slot_ref[...]).astype(jnp.float32).astype(jnp.bfloat16)
    rest = {}

    def home():
        copies[1].wait()
        high, low = split(returned_ref[...])
        rest[0] = dot_tn(placed, high) + dot_tn(placed, low)

    def solved(first, last, inverse):
        x = dot_nt(left(rest[first][:, : last - first], 1), inverse)
        out_ref[:, first:last] = x * factor
        rest[last] = left(x, 1)

    def update(first, last, below):
        rest[last] = rest[first][:, last - first :] - dot_nt(rest[last], below)

    def ready(i, ref):
        copies[i].wait()
        return ref[...]

    steps = [
        home,
        lambda: solved(0, half, ready(2, inverse_ref)),
        lambda: update(0, half, ready(3, across_ref)),
        lambda: solved(half, three, ready(4, next_ref)),
        lambda: update(half, three, ready(5, beyond_ref)),
        lambda: solved(three, three + SIDE, right(tail_ref[:SIDE, :], 1)),
        lambda: update(three, three + SIDE, right(tail_ref[SIDE : 2 * SIDE, :], 1)),
    ]
    copies[0].wait()
    last = invert_factor(tail_ref[2 * SIDE :, :], [lambda: None] * 2 + steps)
    solved(width - SIDE, width, right(last, 1))


SMEM = pl.BlockSpec(memory_space=pltpu.SMEM)
VMEM = pl.BlockSpec(memory_space=pltpu.VMEM)
ANY = pl.BlockSpec(memory_space=pl.ANY)


def kernel_call(kernel, in_specs, out_shape, scratch=(), out_specs=None, mib=16, work=0):
    return pl.pallas_call(
        kernel,
        in_specs=in_specs,
        out_specs=out_specs or jax.tree.map(lambda _: VMEM, out_shape),
        out_shape=out_shape,
        scratch_shapes=list(scratch),
        cost_estimate=pl.CostEstimate(flops=2 * work, bytes_accessed=0, transcendentals=0),
        compiler_params=pltpu.CompilerParams(vmem_limit_bytes=mib << 20),
    )


def swap(x, bit):
    return lax.ppermute(x, "sec", [(i, i ^ bit) for i in range(lax.axis_size("sec"))])


def halve(x, bit):
    upper = (lax.axis_index("sec") // bit) % 2
    half = x.shape[0] // 2
    sent = lax.dynamic_slice_in_dim(x, (1 - upper) * half, half, 0)
    kept = lax.dynamic_slice_in_dim(x, upper * half, half, 0)
    return kept + swap(sent, bit)


def double(x, bit):
    upper = (lax.axis_index("sec") // bit) % 2 == 1
    other = swap(x, bit)
    return jnp.where(
        upper, jnp.concatenate([other, x], axis=0), jnp.concatenate([x, other], axis=0)
    )


def reduce_shares(share):
    bits = [1 << b for b in range(1, lax.axis_size("sec").bit_length() - 1)]
    orders = [bits, bits[1:2] + bits[:1] + bits[2:]]
    streams = []
    for order, part in zip(orders, share):
        for bit in order:
            part = halve(part, bit)
        streams.append(part)
    whole = []
    for order, part in zip(orders, streams):
        for bit in reversed(order[1:]):
            part = double(part, bit)
        whole.append((part, order[0]))
    return whole


def per_device(edge_rows, corner, joining, charge_left, charge_right):
    row_count, feature_len = edge_rows.shape
    owners = lax.axis_size("sec")
    capacity = 2 * row_count // owners
    slots = owners * capacity
    factor = math.sqrt(row_count * owners)
    count = feature_len // SIDE
    packed_rows = column_offsets(count)[-1]
    f32, i32 = jnp.float32, jnp.int32
    dma = pltpu.SemaphoreType.DMA
    core = (lax.axis_index("sec") % 2).astype(i32)[None]
    slot, packed = kernel_call(
        functools.partial(route_kernel, capacity),
        [ANY] * 4,
        (
            jax.ShapeDtypeStruct((1, row_count), i32),
            jax.ShapeDtypeStruct((slots, feature_len), edge_rows.dtype),
        ),
        [
            pltpu.VMEM((row_count, feature_len), edge_rows.dtype),
            pltpu.VMEM(joining.shape, i32),
            pltpu.VMEM((1, row_count), i32),
            pltpu.VMEM((1, row_count), i32),
            dma((4,)),
        ],
        mib=60,
    )(edge_rows, joining, charge_left[None, :], charge_right[None, :])
    arrived = lax.all_to_all(
        packed.reshape(owners, capacity, feature_len), "sec", split_axis=0, concat_axis=0, tiled=True
    ).reshape(slots, feature_len)
    corners = kernel_call(
        fetch_kernel,
        [ANY] * 2,
        (jax.ShapeDtypeStruct(corner.shape, corner.dtype),) * 2,
        [dma((2,))],
        work=slots * feature_len * feature_len,
        mib=16,
    )(corner, swap(corner, 1))
    product, share = kernel_call(
        images_kernel,
        [SMEM] + [VMEM] * 4,
        (
            jax.ShapeDtypeStruct((slots, feature_len), f32),
            jax.ShapeDtypeStruct((sum(share_rows(count)), SIDE), f32),
        ),
    )(core, arrived, swap(arrived, 1), *corners)
    streams = reduce_shares(jnp.split(share, [share_rows(count)[0]], axis=0))
    (product, first), second = lax.optimization_barrier(((product, streams[0][0]), streams[1][0]))
    streams = [(first, streams[0][1]), (second, streams[1][1])]
    parts = [double(part, bit) for part, bit in streams]
    returned = lax.all_to_all(
        product.reshape(owners, capacity, feature_len), "sec", split_axis=0, concat_axis=0, tiled=True
    )
    half, quarter = feature_len // 2, feature_len // 4
    lower = kernel_call(
        functools.partial(cholesky_kernel, count),
        [SMEM] + [ANY] * 4,
        (
            jax.ShapeDtypeStruct((half, 3 * half), jnp.bfloat16),
            jax.ShapeDtypeStruct((half, 3 * half), jnp.bfloat16),
            jax.ShapeDtypeStruct((quarter, 3 * quarter), jnp.bfloat16),
            jax.ShapeDtypeStruct((quarter, 3 * quarter), jnp.bfloat16),
            jax.ShapeDtypeStruct((3 * SIDE, SIDE), f32),
        ),
        [
            pltpu.VMEM((packed_rows, SIDE), f32),
            pltpu.VMEM((2, 8, SIDE), f32),
            pltpu.VMEM((half, 3 * half), jnp.bfloat16),
            pltpu.VMEM((half, 3 * half), jnp.bfloat16),
            pltpu.VMEM((quarter, 3 * quarter), jnp.bfloat16),
            pltpu.VMEM((quarter, 3 * quarter), jnp.bfloat16),
            dma((2, 8)),
            dma((5,)),
        ],
        (ANY,) * 5,
        mib=60,
        work=20 * packed_rows * feature_len * feature_len,
    )(core, *parts, *[swap(part, 1) for part in parts])
    returned, lower = lax.optimization_barrier((returned, lower))
    return kernel_call(
        functools.partial(solve_kernel, count, factor),
        [VMEM] + [ANY] * 6,
        jax.ShapeDtypeStruct((row_count, feature_len), f32),
        [
            pltpu.VMEM((3 * SIDE, SIDE), f32),
            pltpu.VMEM((slots, feature_len), f32),
            pltpu.VMEM((half, 3 * half), jnp.bfloat16),
            pltpu.VMEM((half, 3 * half), jnp.bfloat16),
            pltpu.VMEM((quarter, 3 * quarter), jnp.bfloat16),
            pltpu.VMEM((quarter, 3 * quarter), jnp.bfloat16),
            dma((6,)),
        ],
        mib=60,
    )(slot, lower[4], returned.reshape(slots, feature_len), *lower[:4])


def solution(mesh):
    placed = (
        P(("runs", "sec"), None),
        P(("runs", "sec"), None),
        P("runs", None),
        P(("runs", "sec")),
        P(("runs", "sec")),
    )
    return jax.shard_map(
        per_device, mesh=mesh, in_specs=placed, out_specs=P(("runs", "sec"), None), check_vma=False
    )
```

```python
import functools
import math

import jax
import jax.numpy as jnp
from jax import lax
from jax.experimental import pallas as pl
from jax.experimental.pallas import tpu as pltpu
from jax.sharding import PartitionSpec as P

SIDE = 128
LARGE = 32 << 20


def column_offsets(count):
    offsets = [0]
    for j in range(count):
        offsets.append(offsets[-1] + (count - j) * SIDE)
    return offsets


def split(x):
    high = x.astype(jnp.bfloat16)
    return high, (x - high.astype(jnp.float32)).astype(jnp.bfloat16)


def left(x, axis):
    high, low = split(x)
    return jnp.concatenate([high, high, low], axis=axis)


def right(x, axis):
    high, low = split(x)
    return jnp.concatenate([high, low, high], axis=axis)


def dot_nt(a, b):
    return lax.dot_general(a, b, (((1,), (1,)), ((), ())), preferred_element_type=jnp.float32)


def dot_tn(a, b):
    return lax.dot_general(a, b, (((0,), (0,)), ((), ())), preferred_element_type=jnp.float32)


def dot_nn(a, b):
    return jnp.dot(a, b, preferred_element_type=jnp.float32)


def iota(shape, axis):
    return lax.broadcasted_iota(jnp.int32, shape, axis)


def route_kernel(
    capacity, edge_hbm, joining_hbm, left_hbm, right_hbm, slot_ref, packed_ref,
    edge_ref, joining_ref, left_ref, right_ref, done,
):
    bf16 = jnp.bfloat16
    pairs = [
        (joining_hbm, joining_ref),
        (left_hbm, left_ref),
        (right_hbm, right_ref),
        (edge_hbm, edge_ref),
    ]
    copies = [pltpu.make_async_copy(a, b, done.at[i]) for i, (a, b) in enumerate(pairs)]
    for copy in copies:
        copy.start()
    rows = edge_ref.shape[0]
    owners = joining_ref.shape[0]
    slots = packed_ref.shape[0]
    one = lambda hit: hit.astype(jnp.float32)
    label = iota((owners, rows), 0)
    for copy in copies[:3]:
        copy.wait()
    is_left = one(label == left_ref[...]).astype(bf16)
    options = dot_tn(joining_ref[...].astype(jnp.float32).astype(bf16), is_left)
    target = jnp.sum(jnp.where(label == right_ref[...], options, 0.0), axis=0, keepdims=True)
    is_target = label.astype(jnp.float32) == target
    earlier = one(iota((rows, rows), 0) < iota((rows, rows), 1)).astype(bf16)
    before = jnp.dot(one(is_target).astype(bf16), earlier, preferred_element_type=jnp.float32)
    order = jnp.sum(jnp.where(is_target, before, 0.0), axis=0, keepdims=True)
    slot = (target * capacity + order).astype(jnp.int32)
    slot_ref[...] = slot
    placed = one(iota((slots, rows), 0) == slot).astype(bf16)
    copies[3].wait()
    packed_ref[...] = jnp.dot(
        placed, edge_ref[...], preferred_element_type=jnp.float32
    ).astype(bf16)


def fetch_kernel(mine_hbm, other_hbm, mine_ref, other_ref, done):
    copies = [
        pltpu.make_async_copy(mine_hbm, mine_ref, done.at[0]),
        pltpu.make_async_copy(other_hbm, other_ref, done.at[1]),
    ]
    for copy in copies:
        copy.start()
    for copy in copies:
        copy.wait()


def shares(count):
    pairs = list(range(count // 2))
    outer = [p for p in pairs if p % 4 in (0, 3)]
    return outer, [p for p in pairs if p not in outer]


def share_rows(count):
    offsets = column_offsets(count)
    full = (offsets[-1] - count // 2 * SIDE) // 2
    return (full + 128) // 2, full // 2


def images_kernel(
    core_ref, arrived_ref, other_arrived_ref, corner_ref, other_corner_ref, images_ref, gram_ref
):
    width = corner_ref.shape[1]
    count = width // SIDE
    others = dot_nn(other_arrived_ref[...], other_corner_ref[...])
    images = dot_nn(arrived_ref[...], corner_ref[...])
    images_ref[...] = images
    images = jnp.concatenate([images, others], axis=0)
    high, low = split(images)
    second = jnp.concatenate([high, low, high], axis=0)
    high, low = high.T, low.T
    first = jnp.concatenate([high, high, low], axis=1)
    row, col = iota((SIDE, SIDE), 0), iota((SIDE, SIDE), 1)

    def store(at, x):
        gram_ref[at : at + x.shape[0], :] = x

    def share(pairs):
        at = 0
        diagonals = []
        for p in pairs:
            start = 2 * p * SIDE
            part = dot_nn(first[start:], second[:, start : start + 2 * SIDE])
            upper, lower = part[:SIDE, :SIDE], part[SIDE : 2 * SIDE, SIDE:]
            store(at, jnp.where(row >= col, upper, lower))
            store(at + SIDE, part[SIDE : 2 * SIDE, :SIDE])
            diagonals.append(jnp.sum(jnp.where(row == col, lower, 0.0), axis=0, keepdims=True))
            at += 2 * SIDE
            rest = width - start - 2 * SIDE
            if rest:
                store(at, part[2 * SIDE :, :SIDE])
                store(at + rest, part[2 * SIDE :, SIDE:])
                at += 2 * rest
        store(at, jnp.zeros((gram_ref.shape[0] - at, SIDE), jnp.float32))
        for i, diagonal in enumerate(diagonals):
            store(at + i, diagonal)

    for core, pairs in enumerate(shares(count)):
        pl.when(core_ref[0] == core)(functools.partial(share, pairs))


def unpack_share(count, core, parts, lower_ref, diagonal_ref, done):
    offsets = column_offsets(count)
    cut = parts[0].shape[0]
    copies = []

    def copy(target, source, rows):
        for ref, low in ((parts[0], 0), (parts[1], cut)):
            begin, end = max(source, low), min(source + rows, low + ref.shape[0])
            if begin < end:
                copies.append(
                    pltpu.make_async_copy(
                        ref.at[begin - low : end - low],
                        lower_ref.at[target + begin - source : target + end - source],
                        done.at[core, len(copies)],
                    )
                )

    at = 0
    for p in shares(count)[core]:
        first, second = offsets[2 * p], offsets[2 * p + 1]
        rest = (count - 2 * p - 2) * SIDE
        copy(first, at, 2 * SIDE)
        if rest:
            copy(first + 2 * SIDE, at + 2 * SIDE, rest)
            copy(second + SIDE, at + 2 * SIDE + rest, rest)
        at += 2 * SIDE + 2 * rest
    copies.append(
        pltpu.make_async_copy(
            parts[1].at[at - cut : at - cut + 8], diagonal_ref.at[core], done.at[core, len(copies)]
        )
    )
    return copies


def part_diagonals(count, core, lower_ref, diagonal_ref, which):
    offsets = column_offsets(count)
    row, col = iota((SIDE, SIDE), 0), iota((SIDE, SIDE), 1)
    for i, p in list(enumerate(shares(count)[core]))[which]:
        first, second = offsets[2 * p], offsets[2 * p + 1]
        both = lower_ref[first : first + SIDE, :]
        turned = both.T
        diagonal = diagonal_ref[core, i : i + 1, :]
        lower_ref[first : first + SIDE, :] = jnp.where(row >= col, both, turned)
        lower_ref[second : second + SIDE, :] = jnp.where(
            row == col, diagonal, jnp.where(row < col, both, turned)
        )


NEAR = 2


def eliminate(rows, start, tick):
    shape = rows[0].shape
    lane, sub = iota(shape, 1), iota(shape, 0)
    rows = list(rows)
    groups = len(rows)

    def spread(x):
        return jnp.broadcast_to(x, shape)

    def columns_of(x, first):
        return [spread(x[:, first + j : first + j + 1]) for j in range(8)]

    pivots = columns_of(rows[0], start)
    for m in range(groups):
        g = start + 8 * m
        later = range(m + 1, min(groups, m + 1 + NEAR))
        far = range(m + 1 + NEAR, groups)
        inside = (lane >= g) & (lane < g + 8)
        current = rows[m]
        ahead, ahead_below = [], []
        if later:
            ahead = columns_of(current, g + 8)
            ahead_below = columns_of(rows[m + 1], g + 8)
        below = {r: columns_of(rows[r], g) for r in range(m + 1, groups)}
        current = jnp.where(inside, (lane - g == sub).astype(jnp.float32), current)
        for r in range(m + 1, groups):
            rows[r] = jnp.where(inside, 0.0, rows[r])
        diagonal = pivots[0]
        inverses = []
        for j in range(8):
            inverse = 1.0 / spread(pivots[j][j : j + 1, :])
            inverses.append(inverse)
            pivot_row = spread(current[j : j + 1, :])
            heads = [spread(x[j : j + 1, :]) for x in pivots[j + 1 :]]
            ahead_heads = [spread(x[j : j + 1, :]) for x in ahead]
            if j:
                diagonal = jnp.where(sub == j, pivots[j], diagonal)
            if j < 7:
                weight = jnp.where(sub > j, pivots[j], 0.0) * inverse
                current = current - weight * pivot_row
                for k, head in enumerate(heads, j + 1):
                    pivots[k] = pivots[k] - weight * head
                ahead = [x - weight * head for x, head in zip(ahead, ahead_heads)]
            for r in later:
                weight = below[r][j] * inverse
                rows[r] = rows[r] - weight * pivot_row
                for k, head in enumerate(heads, j + 1):
                    below[r][k] = below[r][k] - weight * head
                if r == m + 1:
                    ahead_below = [x - weight * head for x, head in zip(ahead_below, ahead_heads)]
        rows[m] = current * lax.rsqrt(diagonal)
        for j in reversed(range(8)):
            if not far:
                break
            solved = spread(current[j : j + 1, :]) * inverses[j]
            if j:
                current = current - jnp.where(sub < j, pivots[j], 0.0) * solved
            for r in far:
                rows[r] = rows[r] - below[r][j] * solved
        pivots = ahead_below
        tick()
    return rows


def invert_factor(block, beside=()):
    size = block.shape[0]
    half = size // 2
    groups = range(0, half, 8)
    ticks = 2 * len(groups)
    pending = [list(beside[t * len(beside) // ticks : (t + 1) * len(beside) // ticks]) for t in range(ticks)]
    pending.reverse()

    def tick():
        for piece in pending.pop():
            piece()

    lane, row = iota((half, size), 1), iota((half, size), 0)
    upper = jnp.concatenate(eliminate([block[g : g + 8, :] for g in groups], 0, tick), axis=0)
    inverse = jnp.where((lane < half) & (lane > row), 0.0, upper)
    lower = jnp.where(lane < half, 0.0, block[half:, :])
    lower = lower - dot_tn(left(upper[:, half:], 0), right(inverse, 0))
    lower = jnp.concatenate(
        eliminate([lower[g : g + 8, :] for g in groups], half, tick), axis=0
    )
    return jnp.concatenate(
        [jnp.where(lane < half, inverse, 0.0), jnp.where(lane <= row + half, lower, 0.0)], axis=0
    )


def join_inverses(low, between, high):
    middle = dot_nn(left(high, 1), right(dot_nn(left(between, 1), right(low, 0)), 0))
    return jnp.concatenate(
        [
            jnp.concatenate([low, jnp.zeros((low.shape[0], high.shape[1]), jnp.float32)], axis=1),
            jnp.concatenate([-middle, high], axis=1),
        ],
        axis=0,
    )


def form_slices(count, forms_ref):
    half, quarter = count // 2 * SIDE, count // 4 * SIDE
    return [
        forms_ref.at[:half],
        forms_ref.at[half : 2 * half],
        forms_ref.at[2 * half : 2 * half + quarter, : 3 * quarter],
        forms_ref.at[2 * half : 2 * half + quarter, 3 * quarter :],
    ]


def cholesky_kernel(
    count, core_ref, mine0, mine1, other0, other1, forms_hbm, tail_hbm,
    lower_ref, diagonal_ref, inverse_ref, across_ref, next_ref, beyond_ref, done, out_done,
):
    offsets = column_offsets(count)
    half, three = count // 2, 3 * count // 4
    for core in (0, 1):

        @pl.when(core_ref[0] == core)
        def _(core=core):
            copies = unpack_share(count, core, (mine0, mine1), lower_ref, diagonal_ref, done)
            copies += unpack_share(count, 1 - core, (other0, other1), lower_ref, diagonal_ref, done)
            for copy in copies:
                copy.start()

    arrivals = [
        unpack_share(count, core, (mine0, mine1), lower_ref, diagonal_ref, done) for core in (0, 1)
    ]
    arrivals[0][0].wait()
    arrivals[0][-1].wait()
    part_diagonals(count, 0, lower_ref, diagonal_ref, slice(0, 1))

    def arrive():
        for copy in arrivals[0][1:-1] + arrivals[1]:
            copy.wait()
        part_diagonals(count, 0, lower_ref, diagonal_ref, slice(1, None))
        part_diagonals(count, 1, lower_ref, diagonal_ref, slice(None))

    def at(i, j):
        first = offsets[j] + (i - j) * SIDE
        return slice(first, first + SIDE)

    def blocks(rows, columns):
        return jnp.concatenate(
            [lower_ref[at(rows[0], j).start : at(rows[-1], j).stop, :] for j in columns], axis=1
        )

    inverses = {}
    outward = []
    form_refs = form_slices(count, forms_hbm)

    def send(ref, hbm):
        outward.append(pltpu.make_async_copy(ref, hbm, out_done.at[len(outward)]))
        outward[-1].start()

    def pair(p):
        def run():
            inverses[p] = join_inverses(
                lower_ref[at(p, p), :], lower_ref[at(p + 1, p), :], lower_ref[at(p + 1, p + 1), :]
            )

        return run

    def join_half():
        inverse_ref[...] = right(
            join_inverses(inverses[0], blocks(range(2, 4), range(2)), inverses[2]), 1
        )
        send(inverse_ref, form_refs[0])

    def across():
        across_ref[...] = right(blocks(range(half, count), range(half)), 1)
        send(across_ref, form_refs[1])

    def beyond():
        next_ref[...] = right(inverses[half], 1)
        beyond_ref[...] = right(blocks(range(three, count), range(half, three)), 1)
        send(next_ref, form_refs[2])
        send(beyond_ref, form_refs[3])

    extra = {2: [pair(0)], 4: [pair(2), join_half, across], 6: [pair(half), beyond]}

    def rest_of(k, head):
        pieces, forms = [], {}
        if k + 2 >= count:
            return pieces
        rest = slice(at(k + 2, k).start, offsets[k + 1])

        def panel():
            below = dot_nt(left(lower_ref[rest, :], 1), right(lower_ref[at(k, k), :], 1))
            lower_ref[rest, :] = below
            forms["left"], forms["right"] = left(below, 1), right(below, 1)

        def next_column():
            lower_ref[at(k + 2, k + 1).start : offsets[k + 2], :] -= dot_nt(
                forms["left"], right(head, 1)
            )

        def product(j, i):
            def run():
                high = min(i + 2, count)
                rows = slice((i - k - 2) * SIDE, (high - k - 2) * SIDE)
                columns = slice((j - k - 2) * SIDE, (min(j + 2, count) - k - 2) * SIDE)
                part = dot_nt(forms["left"][rows], forms["right"][columns])
                lower_ref[at(i, j).start : at(high - 1, j).stop, :] -= part[:, :SIDE]
                if j + 1 < count:
                    skip = SIDE if i == j else 0
                    lower_ref[at(max(i, j + 1), j + 1).start : at(high - 1, j + 1).stop, :] -= part[
                        skip:, SIDE:
                    ]

            return run

        pieces += [panel, next_column]
        for j in range(k + 2, count, 2):
            for i in range(j, count, 2):
                pieces.append(product(j, i))
        return pieces

    beside = [lambda: None] * 2 + [arrive]
    for k in range(count - 1):
        inverse = invert_factor(lower_ref[at(k, k), :], beside + extra.get(k, []))
        lower_ref[at(k, k), :] = inverse
        head = dot_nt(left(lower_ref[at(k + 1, k), :], 1), right(inverse, 1))
        lower_ref[at(k + 1, k), :] = head
        lower_ref[at(k + 1, k + 1), :] -= dot_nt(left(head, 1), right(head, 1))
        beside = rest_of(k, head)
    send(lower_ref.at[offsets[count - 2] :], tail_hbm.at[: 3 * SIDE])
    for copy in outward:
        copy.wait()


def solve_kernel(
    count, factor, slot_ref, tail_hbm, returned_hbm, forms_hbm, out_ref,
    tail_ref, returned_ref, inverse_ref, across_ref, next_ref, beyond_ref, done,
):
    half, three = count // 2 * SIDE, 3 * count // 4 * SIDE
    pairs = [(tail_hbm.at[: 3 * SIDE], tail_ref), (returned_hbm, returned_ref)]
    pairs += zip(form_slices(count, forms_hbm), (inverse_ref, across_ref, next_ref, beyond_ref))
    copies = [pltpu.make_async_copy(a, b, done.at[i]) for i, (a, b) in enumerate(pairs)]
    for copy in copies:
        copy.start()
    slots, rows = returned_ref.shape[0], slot_ref.shape[1]
    width = returned_ref.shape[1]
    placed = (iota((slots, rows), 0) == slot_ref[...]).astype(jnp.float32).astype(jnp.bfloat16)
    rest = {}

    def home():
        copies[1].wait()
        high, low = split(returned_ref[...])
        rest[0] = dot_tn(placed, high) + dot_tn(placed, low)

    def solved(first, last, inverse):
        source = left(rest[first][:, : last - first], 1)
        if last - first == half:
            cut = half // 2
            short = [slice(i * half, i * half + cut) for i in range(3)]
            begin = dot_nt(
                jnp.concatenate([source[:, i] for i in short], axis=1),
                jnp.concatenate([inverse[:cut, i] for i in short], axis=1),
            )
            x = jnp.concatenate([begin, dot_nt(source, inverse[cut:])], axis=1)
        else:
            x = dot_nt(source, inverse)
        out_ref[:, first:last] = x * factor
        rest[last] = left(x, 1)

    def update(first, last, below):
        rest[last] = rest[first][:, last - first :] - dot_nt(rest[last], below)

    def ready(i, ref):
        copies[i].wait()
        return ref[...]

    steps = [
        home,
        lambda: solved(0, half, ready(2, inverse_ref)),
        lambda: update(0, half, ready(3, across_ref)),
        lambda: solved(half, three, ready(4, next_ref)),
        lambda: update(half, three, ready(5, beyond_ref)),
        lambda: solved(three, three + SIDE, right(tail_ref[:SIDE, :], 1)),
        lambda: update(three, three + SIDE, right(tail_ref[SIDE : 2 * SIDE, :], 1)),
    ]
    copies[0].wait()
    last = invert_factor(tail_ref[2 * SIDE :, :], [lambda: None] * 2 + steps)
    solved(width - SIDE, width, right(last, 1))


SMEM = pl.BlockSpec(memory_space=pltpu.SMEM)
VMEM = pl.BlockSpec(memory_space=pltpu.VMEM)
ANY = pl.BlockSpec(memory_space=pl.ANY)


def kernel_call(kernel, in_specs, out_shape, scratch=(), out_specs=None, mib=16, work=0):
    return pl.pallas_call(
        kernel,
        in_specs=in_specs,
        out_specs=out_specs or jax.tree.map(lambda _: VMEM, out_shape),
        out_shape=out_shape,
        scratch_shapes=list(scratch),
        cost_estimate=pl.CostEstimate(flops=2 * work, bytes_accessed=0, transcendentals=0),
        compiler_params=pltpu.CompilerParams(vmem_limit_bytes=mib << 20),
    )


def swap(x, bit):
    return lax.ppermute(x, "sec", [(i, i ^ bit) for i in range(lax.axis_size("sec"))])


def halve(x, bit):
    upper = (lax.axis_index("sec") // bit) % 2
    half = x.shape[0] // 2
    sent = lax.dynamic_slice_in_dim(x, (1 - upper) * half, half, 0)
    kept = lax.dynamic_slice_in_dim(x, upper * half, half, 0)
    return kept + swap(sent, bit)


def double(x, bit):
    upper = (lax.axis_index("sec") // bit) % 2 == 1
    other = swap(x, bit)
    return jnp.where(
        upper, jnp.concatenate([other, x], axis=0), jnp.concatenate([x, other], axis=0)
    )


def reduce_shares(share):
    bits = [1 << b for b in range(1, lax.axis_size("sec").bit_length() - 1)]
    orders = [bits, bits[1:2] + bits[:1] + bits[2:]]
    streams = []
    for order, part in zip(orders, share):
        for bit in order:
            part = halve(part, bit)
        streams.append(part)
    whole = []
    for order, part in zip(orders, streams):
        for bit in reversed(order[1:]):
            part = double(part, bit)
        whole.append((part, order[0]))
    return whole


def per_device(edge_rows, corner, joining, charge_left, charge_right):
    row_count, feature_len = edge_rows.shape
    owners = lax.axis_size("sec")
    capacity = 2 * row_count // owners
    slots = owners * capacity
    factor = math.sqrt(row_count * owners)
    count = feature_len // SIDE
    packed_rows = column_offsets(count)[-1]
    f32, i32 = jnp.float32, jnp.int32
    dma = pltpu.SemaphoreType.DMA
    core = (lax.axis_index("sec") % 2).astype(i32)[None]
    slot, packed = kernel_call(
        functools.partial(route_kernel, capacity),
        [ANY] * 4,
        (
            jax.ShapeDtypeStruct((1, row_count), i32),
            jax.ShapeDtypeStruct((slots, feature_len), edge_rows.dtype),
        ),
        [
            pltpu.VMEM((row_count, feature_len), edge_rows.dtype),
            pltpu.VMEM(joining.shape, i32),
            pltpu.VMEM((1, row_count), i32),
            pltpu.VMEM((1, row_count), i32),
            dma((4,)),
        ],
        mib=60,
    )(edge_rows, joining, charge_left[None, :], charge_right[None, :])
    arrived = lax.all_to_all(
        packed.reshape(owners, capacity, feature_len), "sec", split_axis=0, concat_axis=0, tiled=True
    ).reshape(slots, feature_len)
    corners = kernel_call(
        fetch_kernel,
        [ANY] * 2,
        (jax.ShapeDtypeStruct(corner.shape, corner.dtype),) * 2,
        [dma((2,))],
        work=slots * feature_len * feature_len,
        mib=16,
    )(corner, swap(corner, 1))
    product, share = kernel_call(
        images_kernel,
        [SMEM] + [VMEM] * 4,
        (
            jax.ShapeDtypeStruct((slots, feature_len), f32),
            jax.ShapeDtypeStruct((sum(share_rows(count)), SIDE), f32),
        ),
    )(core, arrived, swap(arrived, 1), *corners)
    streams = reduce_shares(jnp.split(share, [share_rows(count)[0]], axis=0))
    (product, first), second = lax.optimization_barrier(((product, streams[0][0]), streams[1][0]))
    streams = [(first, streams[0][1]), (second, streams[1][1])]
    parts = [double(part, bit) for part, bit in streams]
    returned = lax.all_to_all(
        product.reshape(owners, capacity, feature_len), "sec", split_axis=0, concat_axis=0, tiled=True
    )
    half, quarter = feature_len // 2, feature_len // 4
    lower = kernel_call(
        functools.partial(cholesky_kernel, count),
        [SMEM] + [ANY] * 4,
        (
            jax.ShapeDtypeStruct((LARGE // 6 // half, 3 * half), jnp.bfloat16),
            jax.ShapeDtypeStruct((LARGE // 4 // SIDE, SIDE), f32),
        ),
        [
            pltpu.VMEM((packed_rows, SIDE), f32),
            pltpu.VMEM((2, 8, SIDE), f32),
            pltpu.VMEM((half, 3 * half), jnp.bfloat16),
            pltpu.VMEM((half, 3 * half), jnp.bfloat16),
            pltpu.VMEM((quarter, 3 * quarter), jnp.bfloat16),
            pltpu.VMEM((quarter, 3 * quarter), jnp.bfloat16),
            dma((2, 8)),
            dma((5,)),
        ],
        (ANY,) * 2,
        mib=44,
        work=20 * packed_rows * feature_len * feature_len,
    )(core, *parts, *[swap(part, 1) for part in parts])
    returned, lower = lax.optimization_barrier((returned, lower))
    return kernel_call(
        functools.partial(solve_kernel, count, factor),
        [VMEM] + [ANY] * 3,
        jax.ShapeDtypeStruct((row_count, feature_len), f32),
        [
            pltpu.VMEM((3 * SIDE, SIDE), f32),
            pltpu.VMEM((slots, feature_len), f32),
            pltpu.VMEM((half, 3 * half), jnp.bfloat16),
            pltpu.VMEM((half, 3 * half), jnp.bfloat16),
            pltpu.VMEM((quarter, 3 * quarter), jnp.bfloat16),
            pltpu.VMEM((quarter, 3 * quarter), jnp.bfloat16),
            dma((6,)),
        ],
        mib=60,
    )(slot, lower[1], returned.reshape(slots, feature_len), lower[0])


def solution(mesh):
    placed = (
        P(("runs", "sec"), None),
        P(("runs", "sec"), None),
        P("runs", None),
        P(("runs", "sec")),
        P(("runs", "sec")),
    )
    return jax.shard_map(
        per_device, mesh=mesh, in_specs=placed, out_specs=P(("runs", "sec"), None), check_vma=False
    )
```

```python
import functools
import math

import jax
import jax.numpy as jnp
from jax import lax
from jax.experimental import pallas as pl
from jax.experimental.pallas import tpu as pltpu
from jax.sharding import PartitionSpec as P

SIDE = 128
LARGE = 32 << 20


def column_offsets(count):
    offsets = [0]
    for j in range(count):
        offsets.append(offsets[-1] + (count - j) * SIDE)
    return offsets


def split(x):
    high = x.astype(jnp.bfloat16)
    return high, (x - high.astype(jnp.float32)).astype(jnp.bfloat16)


def left(x, axis):
    high, low = split(x)
    return jnp.concatenate([high, high, low], axis=axis)


def right(x, axis):
    high, low = split(x)
    return jnp.concatenate([high, low, high], axis=axis)


def dot_nt(a, b):
    return lax.dot_general(a, b, (((1,), (1,)), ((), ())), preferred_element_type=jnp.float32)


def dot_tn(a, b):
    return lax.dot_general(a, b, (((0,), (0,)), ((), ())), preferred_element_type=jnp.float32)


def dot_nn(a, b):
    return jnp.dot(a, b, preferred_element_type=jnp.float32)


def iota(shape, axis):
    return lax.broadcasted_iota(jnp.int32, shape, axis)


def route_kernel(
    capacity, edge_hbm, joining_hbm, left_hbm, right_hbm, slot_ref, packed_ref,
    edge_ref, joining_ref, left_ref, right_ref, done,
):
    bf16 = jnp.bfloat16
    pairs = [
        (joining_hbm, joining_ref),
        (left_hbm, left_ref),
        (right_hbm, right_ref),
        (edge_hbm, edge_ref),
    ]
    copies = [pltpu.make_async_copy(a, b, done.at[i]) for i, (a, b) in enumerate(pairs)]
    for copy in copies:
        copy.start()
    rows = edge_ref.shape[0]
    owners = joining_ref.shape[0]
    slots = packed_ref.shape[0]
    one = lambda hit: hit.astype(jnp.float32)
    label = iota((owners, rows), 0)
    for copy in copies[:3]:
        copy.wait()
    is_left = one(label == left_ref[...]).astype(bf16)
    options = dot_tn(joining_ref[...].astype(jnp.float32).astype(bf16), is_left)
    target = jnp.sum(jnp.where(label == right_ref[...], options, 0.0), axis=0, keepdims=True)
    is_target = label.astype(jnp.float32) == target
    earlier = one(iota((rows, rows), 0) < iota((rows, rows), 1)).astype(bf16)
    before = jnp.dot(one(is_target).astype(bf16), earlier, preferred_element_type=jnp.float32)
    order = jnp.sum(jnp.where(is_target, before, 0.0), axis=0, keepdims=True)
    slot = (target * capacity + order).astype(jnp.int32)
    slot_ref[...] = slot
    placed = one(iota((slots, rows), 0) == slot).astype(bf16)
    copies[3].wait()
    packed_ref[...] = jnp.dot(
        placed, edge_ref[...], preferred_element_type=jnp.float32
    ).astype(bf16)


def fetch_kernel(mine_hbm, other_hbm, mine_ref, other_ref, done):
    copies = [
        pltpu.make_async_copy(mine_hbm, mine_ref, done.at[0]),
        pltpu.make_async_copy(other_hbm, other_ref, done.at[1]),
    ]
    for copy in copies:
        copy.start()
    for copy in copies:
        copy.wait()


def shares(count):
    pairs = list(range(count // 2))
    outer = [p for p in pairs if p % 4 in (0, 3)]
    return outer, [p for p in pairs if p not in outer]


def share_rows(count):
    offsets = column_offsets(count)
    full = (offsets[-1] - count // 2 * SIDE) // 2
    return (full + 128) // 2, full // 2


def images_kernel(
    core_ref, arrived_ref, other_arrived_ref, corner_ref, other_corner_ref, images_hbm, gram_ref,
    images_ref, done,
):
    width = corner_ref.shape[1]
    count = width // SIDE
    images = dot_nn(arrived_ref[...], corner_ref[...])
    images_ref[...] = images
    copy = pltpu.make_async_copy(images_ref, images_hbm, done)
    copy.start()
    others = dot_nn(other_arrived_ref[...], other_corner_ref[...])
    images = jnp.concatenate([images, others], axis=0)
    high, low = split(images)
    second = jnp.concatenate([high, low, high], axis=0)
    high, low = high.T, low.T
    first = jnp.concatenate([high, high, low], axis=1)
    row, col = iota((SIDE, SIDE), 0), iota((SIDE, SIDE), 1)

    def store(at, x):
        gram_ref[at : at + x.shape[0], :] = x

    def share(pairs):
        at = 0
        diagonals = []
        for p in pairs:
            start = 2 * p * SIDE
            part = dot_nn(first[start:], second[:, start : start + 2 * SIDE])
            upper, lower = part[:SIDE, :SIDE], part[SIDE : 2 * SIDE, SIDE:]
            store(at, jnp.where(row >= col, upper, lower))
            store(at + SIDE, part[SIDE : 2 * SIDE, :SIDE])
            diagonals.append(jnp.sum(jnp.where(row == col, lower, 0.0), axis=0, keepdims=True))
            at += 2 * SIDE
            rest = width - start - 2 * SIDE
            if rest:
                store(at, part[2 * SIDE :, :SIDE])
                store(at + rest, part[2 * SIDE :, SIDE:])
                at += 2 * rest
        store(at, jnp.zeros((gram_ref.shape[0] - at, SIDE), jnp.float32))
        for i, diagonal in enumerate(diagonals):
            store(at + i, diagonal)

    for core, pairs in enumerate(shares(count)):
        pl.when(core_ref[0] == core)(functools.partial(share, pairs))
    copy.wait()


def unpack_share(count, core, parts, lower_ref, diagonal_ref, done):
    offsets = column_offsets(count)
    cut = parts[0].shape[0]
    copies = []

    def copy(target, source, rows):
        for ref, low in ((parts[0], 0), (parts[1], cut)):
            begin, end = max(source, low), min(source + rows, low + ref.shape[0])
            if begin < end:
                copies.append(
                    pltpu.make_async_copy(
                        ref.at[begin - low : end - low],
                        lower_ref.at[target + begin - source : target + end - source],
                        done.at[core, len(copies)],
                    )
                )

    at = 0
    for p in shares(count)[core]:
        first, second = offsets[2 * p], offsets[2 * p + 1]
        rest = (count - 2 * p - 2) * SIDE
        copy(first, at, 2 * SIDE)
        if rest:
            copy(first + 2 * SIDE, at + 2 * SIDE, rest)
            copy(second + SIDE, at + 2 * SIDE + rest, rest)
        at += 2 * SIDE + 2 * rest
    copies.append(
        pltpu.make_async_copy(
            parts[1].at[at - cut : at - cut + 8], diagonal_ref.at[core], done.at[core, len(copies)]
        )
    )
    return copies


def part_diagonals(count, core, lower_ref, diagonal_ref, which):
    offsets = column_offsets(count)
    row, col = iota((SIDE, SIDE), 0), iota((SIDE, SIDE), 1)
    for i, p in list(enumerate(shares(count)[core]))[which]:
        first, second = offsets[2 * p], offsets[2 * p + 1]
        both = lower_ref[first : first + SIDE, :]
        turned = both.T
        diagonal = diagonal_ref[core, i : i + 1, :]
        lower_ref[first : first + SIDE, :] = jnp.where(row >= col, both, turned)
        lower_ref[second : second + SIDE, :] = jnp.where(
            row == col, diagonal, jnp.where(row < col, both, turned)
        )


NEAR = 2


def eliminate(rows, start, tick):
    shape = rows[0].shape
    lane, sub = iota(shape, 1), iota(shape, 0)
    rows = list(rows)
    groups = len(rows)

    def spread(x):
        return jnp.broadcast_to(x, shape)

    def columns_of(x, first):
        return [spread(x[:, first + j : first + j + 1]) for j in range(8)]

    pivots = columns_of(rows[0], start)
    for m in range(groups):
        g = start + 8 * m
        later = range(m + 1, min(groups, m + 1 + NEAR))
        far = range(m + 1 + NEAR, groups)
        inside = (lane >= g) & (lane < g + 8)
        current = rows[m]
        ahead, ahead_below = [], []
        if later:
            ahead = columns_of(current, g + 8)
            ahead_below = columns_of(rows[m + 1], g + 8)
        below = {r: columns_of(rows[r], g) for r in range(m + 1, groups)}
        current = jnp.where(inside, (lane - g == sub).astype(jnp.float32), current)
        for r in range(m + 1, groups):
            rows[r] = jnp.where(inside, 0.0, rows[r])
        diagonal = pivots[0]
        inverses = []
        for j in range(8):
            inverse = 1.0 / spread(pivots[j][j : j + 1, :])
            inverses.append(inverse)
            pivot_row = spread(current[j : j + 1, :])
            heads = [spread(x[j : j + 1, :]) for x in pivots[j + 1 :]]
            ahead_heads = [spread(x[j : j + 1, :]) for x in ahead]
            if j:
                diagonal = jnp.where(sub == j, pivots[j], diagonal)
            if j < 7:
                weight = jnp.where(sub > j, pivots[j], 0.0) * inverse
                current = current - weight * pivot_row
                for k, head in enumerate(heads, j + 1):
                    pivots[k] = pivots[k] - weight * head
                ahead = [x - weight * head for x, head in zip(ahead, ahead_heads)]
            for r in later:
                weight = below[r][j] * inverse
                rows[r] = rows[r] - weight * pivot_row
                for k, head in enumerate(heads, j + 1):
                    below[r][k] = below[r][k] - weight * head
                if r == m + 1:
                    ahead_below = [x - weight * head for x, head in zip(ahead_below, ahead_heads)]
        rows[m] = current * lax.rsqrt(diagonal)
        for j in reversed(range(8)):
            if not far:
                break
            solved = spread(current[j : j + 1, :]) * inverses[j]
            if j:
                current = current - jnp.where(sub < j, pivots[j], 0.0) * solved
            for r in far:
                rows[r] = rows[r] - below[r][j] * solved
        pivots = ahead_below
        tick()
    return rows


def invert_factor(block, beside=()):
    size = block.shape[0]
    half = size // 2
    groups = range(0, half, 8)
    ticks = 2 * len(groups)
    pending = [list(beside[t * len(beside) // ticks : (t + 1) * len(beside) // ticks]) for t in range(ticks)]
    pending.reverse()

    def tick():
        for piece in pending.pop():
            piece()

    lane, row = iota((half, size), 1), iota((half, size), 0)
    upper = jnp.concatenate(eliminate([block[g : g + 8, :] for g in groups], 0, tick), axis=0)
    inverse = jnp.where((lane < half) & (lane > row), 0.0, upper)
    lower = jnp.where(lane < half, 0.0, block[half:, :])
    lower = lower - dot_tn(left(upper[:, half:], 0), right(inverse, 0))
    lower = jnp.concatenate(
        eliminate([lower[g : g + 8, :] for g in groups], half, tick), axis=0
    )
    return jnp.concatenate(
        [jnp.where(lane < half, inverse, 0.0), jnp.where(lane <= row + half, lower, 0.0)], axis=0
    )


def join_inverses(low, between, high):
    middle = dot_nn(left(high, 1), right(dot_nn(left(between, 1), right(low, 0)), 0))
    return jnp.concatenate(
        [
            jnp.concatenate([low, jnp.zeros((low.shape[0], high.shape[1]), jnp.float32)], axis=1),
            jnp.concatenate([-middle, high], axis=1),
        ],
        axis=0,
    )


def form_slices(count, forms_ref):
    half, quarter = count // 2 * SIDE, count // 4 * SIDE
    return [
        forms_ref.at[:half],
        forms_ref.at[half : 2 * half],
        forms_ref.at[2 * half : 2 * half + quarter, : 3 * quarter],
        forms_ref.at[2 * half : 2 * half + quarter, 3 * quarter :],
    ]


def cholesky_kernel(
    count, core_ref, mine0, mine1, other0, other1, forms_hbm, tail_hbm,
    lower_ref, diagonal_ref, inverse_ref, across_ref, next_ref, beyond_ref, done, out_done,
):
    offsets = column_offsets(count)
    half, three = count // 2, 3 * count // 4
    for core in (0, 1):

        @pl.when(core_ref[0] == core)
        def _(core=core):
            copies = unpack_share(count, core, (mine0, mine1), lower_ref, diagonal_ref, done)
            copies += unpack_share(count, 1 - core, (other0, other1), lower_ref, diagonal_ref, done)
            for copy in copies:
                copy.start()

    arrivals = [
        unpack_share(count, core, (mine0, mine1), lower_ref, diagonal_ref, done) for core in (0, 1)
    ]
    arrivals[0][0].wait()
    arrivals[0][-1].wait()
    part_diagonals(count, 0, lower_ref, diagonal_ref, slice(0, 1))

    def arrive():
        for copy in arrivals[0][1:-1] + arrivals[1]:
            copy.wait()
        part_diagonals(count, 0, lower_ref, diagonal_ref, slice(1, None))
        part_diagonals(count, 1, lower_ref, diagonal_ref, slice(None))

    def at(i, j):
        first = offsets[j] + (i - j) * SIDE
        return slice(first, first + SIDE)

    def blocks(rows, columns):
        return jnp.concatenate(
            [lower_ref[at(rows[0], j).start : at(rows[-1], j).stop, :] for j in columns], axis=1
        )

    inverses = {}
    outward = []
    form_refs = form_slices(count, forms_hbm)

    def send(ref, hbm):
        outward.append(pltpu.make_async_copy(ref, hbm, out_done.at[len(outward)]))
        outward[-1].start()

    def pair(p):
        def run():
            inverses[p] = join_inverses(
                lower_ref[at(p, p), :], lower_ref[at(p + 1, p), :], lower_ref[at(p + 1, p + 1), :]
            )

        return run

    def join_half():
        inverse_ref[...] = right(
            join_inverses(inverses[0], blocks(range(2, 4), range(2)), inverses[2]), 1
        )
        send(inverse_ref, form_refs[0])

    def across():
        across_ref[...] = right(blocks(range(half, count), range(half)), 1)
        send(across_ref, form_refs[1])

    def beyond():
        next_ref[...] = right(inverses[half], 1)
        beyond_ref[...] = right(blocks(range(three, count), range(half, three)), 1)
        send(next_ref, form_refs[2])
        send(beyond_ref, form_refs[3])

    extra = {2: [pair(0)], 4: [pair(2), join_half, across], 6: [pair(half), beyond]}

    def rest_of(k, head):
        pieces, forms = [], {}
        if k + 2 >= count:
            return pieces
        rest = slice(at(k + 2, k).start, offsets[k + 1])

        def panel():
            below = dot_nt(left(lower_ref[rest, :], 1), right(lower_ref[at(k, k), :], 1))
            lower_ref[rest, :] = below
            forms["left"], forms["right"] = left(below, 1), right(below, 1)

        def next_column():
            lower_ref[at(k + 2, k + 1).start : offsets[k + 2], :] -= dot_nt(
                forms["left"], right(head, 1)
            )

        def product(j, i):
            def run():
                high = min(i + 2, count)
                rows = slice((i - k - 2) * SIDE, (high - k - 2) * SIDE)
                columns = slice((j - k - 2) * SIDE, (min(j + 2, count) - k - 2) * SIDE)
                part = dot_nt(forms["left"][rows], forms["right"][columns])
                lower_ref[at(i, j).start : at(high - 1, j).stop, :] -= part[:, :SIDE]
                if j + 1 < count:
                    skip = SIDE if i == j else 0
                    lower_ref[at(max(i, j + 1), j + 1).start : at(high - 1, j + 1).stop, :] -= part[
                        skip:, SIDE:
                    ]

            return run

        pieces += [panel, next_column]
        for j in range(k + 2, count, 2):
            for i in range(j, count, 2):
                pieces.append(product(j, i))
        return pieces

    beside = [lambda: None] * 2 + [arrive]
    for k in range(count - 1):
        inverse = invert_factor(lower_ref[at(k, k), :], beside + extra.get(k, []))
        lower_ref[at(k, k), :] = inverse
        head = dot_nt(left(lower_ref[at(k + 1, k), :], 1), right(inverse, 1))
        lower_ref[at(k + 1, k), :] = head
        lower_ref[at(k + 1, k + 1), :] -= dot_nt(left(head, 1), right(head, 1))
        beside = rest_of(k, head)
    send(lower_ref.at[offsets[count - 2] :], tail_hbm.at[: 3 * SIDE])
    for copy in outward:
        copy.wait()


def solve_kernel(
    count, factor, slot_ref, tail_hbm, returned_hbm, forms_hbm, out_hbm,
    tail_ref, returned_ref, inverse_ref, across_ref, next_ref, beyond_ref, out_ref, done, out_done,
):
    half, three = count // 2 * SIDE, 3 * count // 4 * SIDE
    pairs = [(tail_hbm.at[: 3 * SIDE], tail_ref), (returned_hbm, returned_ref)]
    pairs += zip(form_slices(count, forms_hbm), (inverse_ref, across_ref, next_ref, beyond_ref))
    copies = [pltpu.make_async_copy(a, b, done.at[i]) for i, (a, b) in enumerate(pairs)]
    for copy in copies:
        copy.start()
    slots, rows = returned_ref.shape[0], slot_ref.shape[1]
    width = returned_ref.shape[1]
    placed = (iota((slots, rows), 0) == slot_ref[...]).astype(jnp.float32).astype(jnp.bfloat16)
    rest = {}
    leaving = []

    def home():
        copies[1].wait()
        high, low = split(returned_ref[...])
        rest[0] = dot_tn(placed, high) + dot_tn(placed, low)

    def solved(first, last, inverse):
        source = left(rest[first][:, : last - first], 1)
        if last - first == half:
            cut = half // 2
            short = [slice(i * half, i * half + cut) for i in range(3)]
            begin = dot_nt(
                jnp.concatenate([source[:, i] for i in short], axis=1),
                jnp.concatenate([inverse[:cut, i] for i in short], axis=1),
            )
            x = jnp.concatenate([begin, dot_nt(source, inverse[cut:])], axis=1)
        else:
            x = dot_nt(source, inverse)
        out_ref[:, first:last] = x * factor
        leaving.append(
            pltpu.make_async_copy(
                out_ref.at[:, first:last], out_hbm.at[:, first:last], out_done.at[len(leaving)]
            )
        )
        leaving[-1].start()
        rest[last] = left(x, 1)

    def update(first, last, below):
        rest[last] = rest[first][:, last - first :] - dot_nt(rest[last], below)

    def ready(i, ref):
        copies[i].wait()
        return ref[...]

    steps = [
        home,
        lambda: solved(0, half, ready(2, inverse_ref)),
        lambda: update(0, half, ready(3, across_ref)),
        lambda: solved(half, three, ready(4, next_ref)),
        lambda: update(half, three, ready(5, beyond_ref)),
        lambda: solved(three, three + SIDE, right(tail_ref[:SIDE, :], 1)),
        lambda: update(three, three + SIDE, right(tail_ref[SIDE : 2 * SIDE, :], 1)),
    ]
    copies[0].wait()
    last = invert_factor(tail_ref[2 * SIDE :, :], [lambda: None] * 2 + steps)
    solved(width - SIDE, width, right(last, 1))
    for copy in leaving:
        copy.wait()


SMEM = pl.BlockSpec(memory_space=pltpu.SMEM)
VMEM = pl.BlockSpec(memory_space=pltpu.VMEM)
ANY = pl.BlockSpec(memory_space=pl.ANY)


def kernel_call(kernel, in_specs, out_shape, scratch=(), out_specs=None, mib=16, work=0):
    return pl.pallas_call(
        kernel,
        in_specs=in_specs,
        out_specs=out_specs or jax.tree.map(lambda _: VMEM, out_shape),
        out_shape=out_shape,
        scratch_shapes=list(scratch),
        cost_estimate=pl.CostEstimate(flops=2 * work, bytes_accessed=0, transcendentals=0),
        compiler_params=pltpu.CompilerParams(vmem_limit_bytes=mib << 20),
    )


def swap(x, bit):
    return lax.ppermute(x, "sec", [(i, i ^ bit) for i in range(lax.axis_size("sec"))])


def halve(x, bit):
    upper = (lax.axis_index("sec") // bit) % 2
    half = x.shape[0] // 2
    sent = lax.dynamic_slice_in_dim(x, (1 - upper) * half, half, 0)
    kept = lax.dynamic_slice_in_dim(x, upper * half, half, 0)
    return kept + swap(sent, bit)


def double(x, bit):
    upper = (lax.axis_index("sec") // bit) % 2 == 1
    other = swap(x, bit)
    return jnp.where(
        upper, jnp.concatenate([other, x], axis=0), jnp.concatenate([x, other], axis=0)
    )


def reduce_shares(share):
    bits = [1 << b for b in range(1, lax.axis_size("sec").bit_length() - 1)]
    orders = [bits, bits[1:2] + bits[:1] + bits[2:]]
    streams = []
    for order, part in zip(orders, share):
        for bit in order:
            part = halve(part, bit)
        streams.append(part)
    whole = []
    for order, part in zip(orders, streams):
        for bit in reversed(order[1:]):
            part = double(part, bit)
        whole.append((part, order[0]))
    return whole


def per_device(edge_rows, corner, joining, charge_left, charge_right):
    row_count, feature_len = edge_rows.shape
    owners = lax.axis_size("sec")
    capacity = 2 * row_count // owners
    slots = owners * capacity
    factor = math.sqrt(row_count * owners)
    count = feature_len // SIDE
    packed_rows = column_offsets(count)[-1]
    f32, i32 = jnp.float32, jnp.int32
    dma = pltpu.SemaphoreType.DMA
    core = (lax.axis_index("sec") % 2).astype(i32)[None]
    slot, packed = kernel_call(
        functools.partial(route_kernel, capacity),
        [ANY] * 4,
        (
            jax.ShapeDtypeStruct((1, row_count), i32),
            jax.ShapeDtypeStruct((slots, feature_len), edge_rows.dtype),
        ),
        [
            pltpu.VMEM((row_count, feature_len), edge_rows.dtype),
            pltpu.VMEM(joining.shape, i32),
            pltpu.VMEM((1, row_count), i32),
            pltpu.VMEM((1, row_count), i32),
            dma((4,)),
        ],
        mib=60,
    )(edge_rows, joining, charge_left[None, :], charge_right[None, :])
    arrived = lax.all_to_all(
        packed.reshape(owners, capacity, feature_len), "sec", split_axis=0, concat_axis=0, tiled=True
    ).reshape(slots, feature_len)
    corners = kernel_call(
        fetch_kernel,
        [ANY] * 2,
        (jax.ShapeDtypeStruct(corner.shape, corner.dtype),) * 2,
        [dma((2,))],
        work=slots * feature_len * feature_len,
        mib=16,
    )(corner, swap(corner, 1))
    product, share = kernel_call(
        images_kernel,
        [SMEM] + [VMEM] * 4,
        (
            jax.ShapeDtypeStruct((slots, feature_len), f32),
            jax.ShapeDtypeStruct((sum(share_rows(count)), SIDE), f32),
        ),
        [pltpu.VMEM((slots, feature_len), f32), dma],
        (ANY, VMEM),
    )(core, arrived, swap(arrived, 1), *corners)
    streams = reduce_shares(jnp.split(share, [share_rows(count)[0]], axis=0))
    (product, first), second = lax.optimization_barrier(((product, streams[0][0]), streams[1][0]))
    streams = [(first, streams[0][1]), (second, streams[1][1])]
    parts = [double(part, bit) for part, bit in streams]
    returned = lax.all_to_all(
        product.reshape(owners, capacity, feature_len), "sec", split_axis=0, concat_axis=0, tiled=True
    )
    half, quarter = feature_len // 2, feature_len // 4
    lower = kernel_call(
        functools.partial(cholesky_kernel, count),
        [SMEM] + [ANY] * 4,
        (
            jax.ShapeDtypeStruct((LARGE // 6 // half, 3 * half), jnp.bfloat16),
            jax.ShapeDtypeStruct((LARGE // 4 // SIDE, SIDE), f32),
        ),
        [
            pltpu.VMEM((packed_rows, SIDE), f32),
            pltpu.VMEM((2, 8, SIDE), f32),
            pltpu.VMEM((half, 3 * half), jnp.bfloat16),
            pltpu.VMEM((half, 3 * half), jnp.bfloat16),
            pltpu.VMEM((quarter, 3 * quarter), jnp.bfloat16),
            pltpu.VMEM((quarter, 3 * quarter), jnp.bfloat16),
            dma((2, 8)),
            dma((5,)),
        ],
        (ANY,) * 2,
        mib=44,
        work=20 * packed_rows * feature_len * feature_len,
    )(core, *parts, *[swap(part, 1) for part in parts])
    returned, lower = lax.optimization_barrier((returned, lower))
    return kernel_call(
        functools.partial(solve_kernel, count, factor),
        [VMEM] + [ANY] * 3,
        jax.ShapeDtypeStruct((row_count, feature_len), f32),
        [
            pltpu.VMEM((3 * SIDE, SIDE), f32),
            pltpu.VMEM((slots, feature_len), f32),
            pltpu.VMEM((half, 3 * half), jnp.bfloat16),
            pltpu.VMEM((half, 3 * half), jnp.bfloat16),
            pltpu.VMEM((quarter, 3 * quarter), jnp.bfloat16),
            pltpu.VMEM((quarter, 3 * quarter), jnp.bfloat16),
            pltpu.VMEM((row_count, feature_len), f32),
            dma((6,)),
            dma((4,)),
        ],
        ANY,
        mib=60,
    )(slot, lower[1], returned.reshape(slots, feature_len), lower[0])


def solution(mesh):
    placed = (
        P(("runs", "sec"), None),
        P(("runs", "sec"), None),
        P("runs", None),
        P(("runs", "sec")),
        P(("runs", "sec")),
    )
    return jax.shard_map(
        per_device, mesh=mesh, in_specs=placed, out_specs=P(("runs", "sec"), None), check_vma=False
    )
```

```python
import functools
import math

import jax
import jax.numpy as jnp
from jax import lax
from jax.experimental import pallas as pl
from jax.experimental.pallas import tpu as pltpu
from jax.sharding import PartitionSpec as P

SIDE = 128
LARGE = 32 << 20


def column_offsets(count):
    offsets = [0]
    for j in range(count):
        offsets.append(offsets[-1] + (count - j) * SIDE)
    return offsets


def split(x):
    high = x.astype(jnp.bfloat16)
    return high, (x - high.astype(jnp.float32)).astype(jnp.bfloat16)


def left(x, axis):
    high, low = split(x)
    return jnp.concatenate([high, high, low], axis=axis)


def right(x, axis):
    high, low = split(x)
    return jnp.concatenate([high, low, high], axis=axis)


def dot_nt(a, b):
    return lax.dot_general(a, b, (((1,), (1,)), ((), ())), preferred_element_type=jnp.float32)


def dot_tn(a, b):
    return lax.dot_general(a, b, (((0,), (0,)), ((), ())), preferred_element_type=jnp.float32)


def dot_nn(a, b):
    return jnp.dot(a, b, preferred_element_type=jnp.float32)


def iota(shape, axis):
    return lax.broadcasted_iota(jnp.int32, shape, axis)


def route_kernel(
    capacity, edge_hbm, joining_hbm, left_hbm, right_hbm, slot_ref, packed_hbm,
    packed_ref, edge_ref, joining_ref, left_ref, right_ref, done, out_done,
):
    bf16 = jnp.bfloat16
    pairs = [
        (joining_hbm, joining_ref),
        (left_hbm, left_ref),
        (right_hbm, right_ref),
        (edge_hbm, edge_ref),
    ]
    copies = [pltpu.make_async_copy(a, b, done.at[i]) for i, (a, b) in enumerate(pairs)]
    for copy in copies:
        copy.start()
    rows = edge_ref.shape[0]
    owners = joining_ref.shape[0]
    slots = packed_ref.shape[0]
    one = lambda hit: hit.astype(jnp.float32)
    label = iota((owners, rows), 0)
    for copy in copies[:3]:
        copy.wait()
    is_left = one(label == left_ref[...]).astype(bf16)
    options = dot_tn(joining_ref[...].astype(jnp.float32).astype(bf16), is_left)
    target = jnp.sum(jnp.where(label == right_ref[...], options, 0.0), axis=0, keepdims=True)
    is_target = label.astype(jnp.float32) == target
    earlier = one(iota((rows, rows), 0) < iota((rows, rows), 1)).astype(bf16)
    before = jnp.dot(one(is_target).astype(bf16), earlier, preferred_element_type=jnp.float32)
    order = jnp.sum(jnp.where(is_target, before, 0.0), axis=0, keepdims=True)
    slot = (target * capacity + order).astype(jnp.int32)
    slot_ref[...] = slot
    placed = one(iota((slots, rows), 0) == slot).astype(bf16)
    copies[3].wait()
    half = slots // 2
    leaving = []
    for i, part in enumerate((slice(0, half), slice(half, slots))):
        packed_ref[part, :] = dot_nn(placed[part], edge_ref[...]).astype(bf16)
        leaving.append(
            pltpu.make_async_copy(packed_ref.at[part], packed_hbm.at[part], out_done.at[i])
        )
        leaving[-1].start()
    for copy in leaving:
        copy.wait()


def fetch_kernel(mine_hbm, other_hbm, mine_ref, other_ref, done):
    copies = [
        pltpu.make_async_copy(mine_hbm, mine_ref, done.at[0]),
        pltpu.make_async_copy(other_hbm, other_ref, done.at[1]),
    ]
    for copy in copies:
        copy.start()
    for copy in copies:
        copy.wait()


def shares(count):
    pairs = list(range(count // 2))
    outer = [p for p in pairs if p % 4 in (0, 3)]
    return outer, [p for p in pairs if p not in outer]


def share_rows(count):
    offsets = column_offsets(count)
    full = (offsets[-1] - count // 2 * SIDE) // 2
    return (full + 128) // 2, full // 2


def images_kernel(
    core_ref, arrived_ref, other_arrived_ref, corner_ref, other_corner_ref, images_hbm, gram_ref,
    images_ref, done,
):
    width = corner_ref.shape[1]
    count = width // SIDE
    images = dot_nn(arrived_ref[...], corner_ref[...])
    images_ref[...] = images
    copy = pltpu.make_async_copy(images_ref, images_hbm, done)
    copy.start()
    others = dot_nn(other_arrived_ref[...], other_corner_ref[...])
    images = jnp.concatenate([images, others], axis=0)
    high, low = split(images)
    second = jnp.concatenate([high, low, high], axis=0)
    high, low = high.T, low.T
    first = jnp.concatenate([high, high, low], axis=1)
    row, col = iota((SIDE, SIDE), 0), iota((SIDE, SIDE), 1)

    def store(at, x):
        gram_ref[at : at + x.shape[0], :] = x

    def share(pairs):
        at = 0
        diagonals = []
        for p in pairs:
            start = 2 * p * SIDE
            part = dot_nn(first[start:], second[:, start : start + 2 * SIDE])
            upper, lower = part[:SIDE, :SIDE], part[SIDE : 2 * SIDE, SIDE:]
            store(at, jnp.where(row >= col, upper, lower))
            store(at + SIDE, part[SIDE : 2 * SIDE, :SIDE])
            diagonals.append(jnp.sum(jnp.where(row == col, lower, 0.0), axis=0, keepdims=True))
            at += 2 * SIDE
            rest = width - start - 2 * SIDE
            if rest:
                store(at, part[2 * SIDE :, :SIDE])
                store(at + rest, part[2 * SIDE :, SIDE:])
                at += 2 * rest
        store(at, jnp.zeros((gram_ref.shape[0] - at, SIDE), jnp.float32))
        for i, diagonal in enumerate(diagonals):
            store(at + i, diagonal)

    for core, pairs in enumerate(shares(count)):
        pl.when(core_ref[0] == core)(functools.partial(share, pairs))
    copy.wait()


def unpack_share(count, core, parts, lower_ref, diagonal_ref, done):
    offsets = column_offsets(count)
    cut = parts[0].shape[0]
    copies = []

    def copy(target, source, rows):
        for ref, low in ((parts[0], 0), (parts[1], cut)):
            begin, end = max(source, low), min(source + rows, low + ref.shape[0])
            if begin < end:
                copies.append(
                    pltpu.make_async_copy(
                        ref.at[begin - low : end - low],
                        lower_ref.at[target + begin - source : target + end - source],
                        done.at[core, len(copies)],
                    )
                )

    at = 0
    for p in shares(count)[core]:
        first, second = offsets[2 * p], offsets[2 * p + 1]
        rest = (count - 2 * p - 2) * SIDE
        copy(first, at, 2 * SIDE)
        if rest:
            copy(first + 2 * SIDE, at + 2 * SIDE, rest)
            copy(second + SIDE, at + 2 * SIDE + rest, rest)
        at += 2 * SIDE + 2 * rest
    copies.append(
        pltpu.make_async_copy(
            parts[1].at[at - cut : at - cut + 8], diagonal_ref.at[core], done.at[core, len(copies)]
        )
    )
    return copies


def part_diagonals(count, core, lower_ref, diagonal_ref, which):
    offsets = column_offsets(count)
    row, col = iota((SIDE, SIDE), 0), iota((SIDE, SIDE), 1)
    for i, p in list(enumerate(shares(count)[core]))[which]:
        first, second = offsets[2 * p], offsets[2 * p + 1]
        both = lower_ref[first : first + SIDE, :]
        turned = both.T
        diagonal = diagonal_ref[core, i : i + 1, :]
        lower_ref[first : first + SIDE, :] = jnp.where(row >= col, both, turned)
        lower_ref[second : second + SIDE, :] = jnp.where(
            row == col, diagonal, jnp.where(row < col, both, turned)
        )


NEAR = 2


def eliminate(rows, start, tick):
    shape = rows[0].shape
    lane, sub = iota(shape, 1), iota(shape, 0)
    rows = list(rows)
    groups = len(rows)

    def spread(x):
        return jnp.broadcast_to(x, shape)

    def columns_of(x, first):
        return [spread(x[:, first + j : first + j + 1]) for j in range(8)]

    pivots = columns_of(rows[0], start)
    for m in range(groups):
        g = start + 8 * m
        later = range(m + 1, min(groups, m + 1 + NEAR))
        far = range(m + 1 + NEAR, groups)
        inside = (lane >= g) & (lane < g + 8)
        current = rows[m]
        ahead, ahead_below = [], []
        if later:
            ahead = columns_of(current, g + 8)
            ahead_below = columns_of(rows[m + 1], g + 8)
        below = {r: columns_of(rows[r], g) for r in range(m + 1, groups)}
        current = jnp.where(inside, (lane - g == sub).astype(jnp.float32), current)
        for r in range(m + 1, groups):
            rows[r] = jnp.where(inside, 0.0, rows[r])
        diagonal = pivots[0]
        inverses = []
        for j in range(8):
            inverse = 1.0 / spread(pivots[j][j : j + 1, :])
            inverses.append(inverse)
            pivot_row = spread(current[j : j + 1, :])
            heads = [spread(x[j : j + 1, :]) for x in pivots[j + 1 :]]
            ahead_heads = [spread(x[j : j + 1, :]) for x in ahead]
            if j:
                diagonal = jnp.where(sub == j, pivots[j], diagonal)
            if j < 7:
                weight = jnp.where(sub > j, pivots[j], 0.0) * inverse
                current = current - weight * pivot_row
                for k, head in enumerate(heads, j + 1):
                    pivots[k] = pivots[k] - weight * head
                ahead = [x - weight * head for x, head in zip(ahead, ahead_heads)]
            for r in later:
                weight = below[r][j] * inverse
                rows[r] = rows[r] - weight * pivot_row
                for k, head in enumerate(heads, j + 1):
                    below[r][k] = below[r][k] - weight * head
                if r == m + 1:
                    ahead_below = [x - weight * head for x, head in zip(ahead_below, ahead_heads)]
        rows[m] = current * lax.rsqrt(diagonal)
        for j in reversed(range(8)):
            if not far:
                break
            solved = spread(current[j : j + 1, :]) * inverses[j]
            if j:
                current = current - jnp.where(sub < j, pivots[j], 0.0) * solved
            for r in far:
                rows[r] = rows[r] - below[r][j] * solved
        pivots = ahead_below
        tick()
    return rows


def invert_factor(block, beside=()):
    size = block.shape[0]
    half = size // 2
    groups = range(0, half, 8)
    ticks = 2 * len(groups)
    pending = [list(beside[t * len(beside) // ticks : (t + 1) * len(beside) // ticks]) for t in range(ticks)]
    pending.reverse()

    def tick():
        for piece in pending.pop():
            piece()

    lane, row = iota((half, size), 1), iota((half, size), 0)
    upper = jnp.concatenate(eliminate([block[g : g + 8, :] for g in groups], 0, tick), axis=0)
    inverse = jnp.where((lane < half) & (lane > row), 0.0, upper)
    lower = jnp.where(lane < half, 0.0, block[half:, :])
    lower = lower - dot_tn(left(upper[:, half:], 0), right(inverse, 0))
    lower = jnp.concatenate(
        eliminate([lower[g : g + 8, :] for g in groups], half, tick), axis=0
    )
    return jnp.concatenate(
        [jnp.where(lane < half, inverse, 0.0), jnp.where(lane <= row + half, lower, 0.0)], axis=0
    )


def join_inverses(low, between, high):
    middle = dot_nn(left(high, 1), right(dot_nn(left(between, 1), right(low, 0)), 0))
    return jnp.concatenate(
        [
            jnp.concatenate([low, jnp.zeros((low.shape[0], high.shape[1]), jnp.float32)], axis=1),
            jnp.concatenate([-middle, high], axis=1),
        ],
        axis=0,
    )


def form_slices(count, forms_ref):
    half, quarter = count // 2 * SIDE, count // 4 * SIDE
    return [
        forms_ref.at[:half],
        forms_ref.at[half : 2 * half],
        forms_ref.at[2 * half : 2 * half + quarter, : 3 * quarter],
        forms_ref.at[2 * half : 2 * half + quarter, 3 * quarter :],
    ]


def cholesky_kernel(
    count, core_ref, mine0, mine1, other0, other1, forms_hbm, tail_hbm,
    lower_ref, diagonal_ref, inverse_ref, across_ref, next_ref, beyond_ref, done, out_done,
):
    offsets = column_offsets(count)
    half, three = count // 2, 3 * count // 4
    for core in (0, 1):

        @pl.when(core_ref[0] == core)
        def _(core=core):
            copies = unpack_share(count, core, (mine0, mine1), lower_ref, diagonal_ref, done)
            copies += unpack_share(count, 1 - core, (other0, other1), lower_ref, diagonal_ref, done)
            for copy in copies:
                copy.start()

    arrivals = [
        unpack_share(count, core, (mine0, mine1), lower_ref, diagonal_ref, done) for core in (0, 1)
    ]
    arrivals[0][0].wait()
    arrivals[0][-1].wait()
    part_diagonals(count, 0, lower_ref, diagonal_ref, slice(0, 1))

    def arrive():
        for copy in arrivals[0][1:-1] + arrivals[1]:
            copy.wait()
        part_diagonals(count, 0, lower_ref, diagonal_ref, slice(1, None))
        part_diagonals(count, 1, lower_ref, diagonal_ref, slice(None))

    def at(i, j):
        first = offsets[j] + (i - j) * SIDE
        return slice(first, first + SIDE)

    def blocks(rows, columns):
        return jnp.concatenate(
            [lower_ref[at(rows[0], j).start : at(rows[-1], j).stop, :] for j in columns], axis=1
        )

    inverses = {}
    outward = []
    form_refs = form_slices(count, forms_hbm)

    def send(ref, hbm):
        outward.append(pltpu.make_async_copy(ref, hbm, out_done.at[len(outward)]))
        outward[-1].start()

    def pair(p):
        def run():
            inverses[p] = join_inverses(
                lower_ref[at(p, p), :], lower_ref[at(p + 1, p), :], lower_ref[at(p + 1, p + 1), :]
            )

        return run

    def join_half():
        inverse_ref[...] = right(
            join_inverses(inverses[0], blocks(range(2, 4), range(2)), inverses[2]), 1
        )
        send(inverse_ref, form_refs[0])

    def across():
        across_ref[...] = right(blocks(range(half, count), range(half)), 1)
        send(across_ref, form_refs[1])

    def beyond():
        next_ref[...] = right(inverses[half], 1)
        beyond_ref[...] = right(blocks(range(three, count), range(half, three)), 1)
        send(next_ref, form_refs[2])
        send(beyond_ref, form_refs[3])

    extra = {2: [pair(0)], 4: [pair(2), join_half, across], 6: [pair(half), beyond]}

    def rest_of(k, head):
        pieces, forms = [], {}
        if k + 2 >= count:
            return pieces
        rest = slice(at(k + 2, k).start, offsets[k + 1])

        def panel():
            below = dot_nt(left(lower_ref[rest, :], 1), right(lower_ref[at(k, k), :], 1))
            lower_ref[rest, :] = below
            forms["left"], forms["right"] = left(below, 1), right(below, 1)

        def next_column():
            lower_ref[at(k + 2, k + 1).start : offsets[k + 2], :] -= dot_nt(
                forms["left"], right(head, 1)
            )

        def product(j, i):
            def run():
                high = min(i + 2, count)
                rows = slice((i - k - 2) * SIDE, (high - k - 2) * SIDE)
                columns = slice((j - k - 2) * SIDE, (min(j + 2, count) - k - 2) * SIDE)
                part = dot_nt(forms["left"][rows], forms["right"][columns])
                lower_ref[at(i, j).start : at(high - 1, j).stop, :] -= part[:, :SIDE]
                if j + 1 < count:
                    skip = SIDE if i == j else 0
                    lower_ref[at(max(i, j + 1), j + 1).start : at(high - 1, j + 1).stop, :] -= part[
                        skip:, SIDE:
                    ]

            return run

        pieces += [panel, next_column]
        for j in range(k + 2, count, 2):
            for i in range(j, count, 2):
                pieces.append(product(j, i))
        return pieces

    beside = [lambda: None] * 2 + [arrive]
    for k in range(count - 1):
        inverse = invert_factor(lower_ref[at(k, k), :], beside + extra.get(k, []))
        lower_ref[at(k, k), :] = inverse
        head = dot_nt(left(lower_ref[at(k + 1, k), :], 1), right(inverse, 1))
        lower_ref[at(k + 1, k), :] = head
        lower_ref[at(k + 1, k + 1), :] -= dot_nt(left(head, 1), right(head, 1))
        beside = rest_of(k, head)
    send(lower_ref.at[offsets[count - 2] :], tail_hbm.at[: 3 * SIDE])
    for copy in outward:
        copy.wait()


def solve_kernel(
    count, factor, slot_ref, tail_hbm, returned_hbm, forms_hbm, out_hbm,
    tail_ref, returned_ref, inverse_ref, across_ref, next_ref, beyond_ref, out_ref, done, out_done,
):
    half, three = count // 2 * SIDE, 3 * count // 4 * SIDE
    pairs = [(tail_hbm.at[: 3 * SIDE], tail_ref), (returned_hbm, returned_ref)]
    pairs += zip(form_slices(count, forms_hbm), (inverse_ref, across_ref, next_ref, beyond_ref))
    copies = [pltpu.make_async_copy(a, b, done.at[i]) for i, (a, b) in enumerate(pairs)]
    for copy in copies:
        copy.start()
    slots, rows = returned_ref.shape[0], slot_ref.shape[1]
    width = returned_ref.shape[1]
    placed = (iota((slots, rows), 0) == slot_ref[...]).astype(jnp.float32).astype(jnp.bfloat16)
    rest = {}
    leaving = []

    def home():
        copies[1].wait()
        high, low = split(returned_ref[...])
        rest[0] = dot_tn(placed, high) + dot_tn(placed, low)

    def solved(first, last, inverse):
        source = left(rest[first][:, : last - first], 1)
        if last - first == half:
            cut = half // 2
            short = [slice(i * half, i * half + cut) for i in range(3)]
            begin = dot_nt(
                jnp.concatenate([source[:, i] for i in short], axis=1),
                jnp.concatenate([inverse[:cut, i] for i in short], axis=1),
            )
            x = jnp.concatenate([begin, dot_nt(source, inverse[cut:])], axis=1)
        else:
            x = dot_nt(source, inverse)
        out_ref[:, first:last] = x * factor
        leaving.append(
            pltpu.make_async_copy(
                out_ref.at[:, first:last], out_hbm.at[:, first:last], out_done.at[len(leaving)]
            )
        )
        leaving[-1].start()
        rest[last] = left(x, 1)

    def update(first, last, below):
        rest[last] = rest[first][:, last - first :] - dot_nt(rest[last], below)

    def ready(i, ref):
        copies[i].wait()
        return ref[...]

    steps = [
        home,
        lambda: solved(0, half, ready(2, inverse_ref)),
        lambda: update(0, half, ready(3, across_ref)),
        lambda: solved(half, three, ready(4, next_ref)),
        lambda: update(half, three, ready(5, beyond_ref)),
        lambda: solved(three, three + SIDE, right(tail_ref[:SIDE, :], 1)),
        lambda: update(three, three + SIDE, right(tail_ref[SIDE : 2 * SIDE, :], 1)),
    ]
    copies[0].wait()
    last = invert_factor(tail_ref[2 * SIDE :, :], [lambda: None] * 2 + steps)
    solved(width - SIDE, width, right(last, 1))
    for copy in leaving:
        copy.wait()


SMEM = pl.BlockSpec(memory_space=pltpu.SMEM)
VMEM = pl.BlockSpec(memory_space=pltpu.VMEM)
ANY = pl.BlockSpec(memory_space=pl.ANY)


def kernel_call(kernel, in_specs, out_shape, scratch=(), out_specs=None, mib=16, work=0):
    return pl.pallas_call(
        kernel,
        in_specs=in_specs,
        out_specs=out_specs or jax.tree.map(lambda _: VMEM, out_shape),
        out_shape=out_shape,
        scratch_shapes=list(scratch),
        cost_estimate=pl.CostEstimate(flops=2 * work, bytes_accessed=0, transcendentals=0),
        compiler_params=pltpu.CompilerParams(vmem_limit_bytes=mib << 20),
    )


def swap(x, bit):
    return lax.ppermute(x, "sec", [(i, i ^ bit) for i in range(lax.axis_size("sec"))])


def halve(x, bit):
    upper = (lax.axis_index("sec") // bit) % 2
    half = x.shape[0] // 2
    sent = lax.dynamic_slice_in_dim(x, (1 - upper) * half, half, 0)
    kept = lax.dynamic_slice_in_dim(x, upper * half, half, 0)
    return kept + swap(sent, bit)


def double(x, bit):
    upper = (lax.axis_index("sec") // bit) % 2 == 1
    other = swap(x, bit)
    return jnp.where(
        upper, jnp.concatenate([other, x], axis=0), jnp.concatenate([x, other], axis=0)
    )


def reduce_shares(share):
    bits = [1 << b for b in range(1, lax.axis_size("sec").bit_length() - 1)]
    orders = [bits, bits[1:2] + bits[:1] + bits[2:]]
    streams = []
    for order, part in zip(orders, share):
        for bit in order:
            part = halve(part, bit)
        streams.append(part)
    whole = []
    for order, part in zip(orders, streams):
        for bit in reversed(order[1:]):
            part = double(part, bit)
        whole.append((part, order[0]))
    return whole


def per_device(edge_rows, corner, joining, charge_left, charge_right):
    row_count, feature_len = edge_rows.shape
    owners = lax.axis_size("sec")
    capacity = 2 * row_count // owners
    slots = owners * capacity
    factor = math.sqrt(row_count * owners)
    count = feature_len // SIDE
    packed_rows = column_offsets(count)[-1]
    f32, i32 = jnp.float32, jnp.int32
    dma = pltpu.SemaphoreType.DMA
    core = (lax.axis_index("sec") % 2).astype(i32)[None]
    slot, packed = kernel_call(
        functools.partial(route_kernel, capacity),
        [ANY] * 4,
        (
            jax.ShapeDtypeStruct((1, row_count), i32),
            jax.ShapeDtypeStruct((slots, feature_len), edge_rows.dtype),
        ),
        [
            pltpu.VMEM((slots, feature_len), edge_rows.dtype),
            pltpu.VMEM((row_count, feature_len), edge_rows.dtype),
            pltpu.VMEM(joining.shape, i32),
            pltpu.VMEM((1, row_count), i32),
            pltpu.VMEM((1, row_count), i32),
            dma((4,)),
            dma((2,)),
        ],
        (VMEM, ANY),
        mib=60,
    )(edge_rows, joining, charge_left[None, :], charge_right[None, :])
    arrived = lax.all_to_all(
        packed.reshape(owners, capacity, feature_len), "sec", split_axis=0, concat_axis=0, tiled=True
    ).reshape(slots, feature_len)
    corners = kernel_call(
        fetch_kernel,
        [ANY] * 2,
        (jax.ShapeDtypeStruct(corner.shape, corner.dtype),) * 2,
        [dma((2,))],
        work=slots * feature_len * feature_len,
        mib=16,
    )(corner, swap(corner, 1))
    product, share = kernel_call(
        images_kernel,
        [SMEM] + [VMEM] * 4,
        (
            jax.ShapeDtypeStruct((slots, feature_len), f32),
            jax.ShapeDtypeStruct((sum(share_rows(count)), SIDE), f32),
        ),
        [pltpu.VMEM((slots, feature_len), f32), dma],
        (ANY, VMEM),
    )(core, arrived, swap(arrived, 1), *corners)
    streams = reduce_shares(jnp.split(share, [share_rows(count)[0]], axis=0))
    (product, first), second = lax.optimization_barrier(((product, streams[0][0]), streams[1][0]))
    streams = [(first, streams[0][1]), (second, streams[1][1])]
    parts = [double(part, bit) for part, bit in streams]
    returned = lax.all_to_all(
        product.reshape(owners, capacity, feature_len), "sec", split_axis=0, concat_axis=0, tiled=True
    )
    half, quarter = feature_len // 2, feature_len // 4
    lower = kernel_call(
        functools.partial(cholesky_kernel, count),
        [SMEM] + [ANY] * 4,
        (
            jax.ShapeDtypeStruct((LARGE // 6 // half, 3 * half), jnp.bfloat16),
            jax.ShapeDtypeStruct((LARGE // 4 // SIDE, SIDE), f32),
        ),
        [
            pltpu.VMEM((packed_rows, SIDE), f32),
            pltpu.VMEM((2, 8, SIDE), f32),
            pltpu.VMEM((half, 3 * half), jnp.bfloat16),
            pltpu.VMEM((half, 3 * half), jnp.bfloat16),
            pltpu.VMEM((quarter, 3 * quarter), jnp.bfloat16),
            pltpu.VMEM((quarter, 3 * quarter), jnp.bfloat16),
            dma((2, 8)),
            dma((5,)),
        ],
        (ANY,) * 2,
        mib=44,
        work=20 * packed_rows * feature_len * feature_len,
    )(core, *parts, *[swap(part, 1) for part in parts])
    returned, lower = lax.optimization_barrier((returned, lower))
    return kernel_call(
        functools.partial(solve_kernel, count, factor),
        [VMEM] + [ANY] * 3,
        jax.ShapeDtypeStruct((row_count, feature_len), f32),
        [
            pltpu.VMEM((3 * SIDE, SIDE), f32),
            pltpu.VMEM((slots, feature_len), f32),
            pltpu.VMEM((half, 3 * half), jnp.bfloat16),
            pltpu.VMEM((half, 3 * half), jnp.bfloat16),
            pltpu.VMEM((quarter, 3 * quarter), jnp.bfloat16),
            pltpu.VMEM((quarter, 3 * quarter), jnp.bfloat16),
            pltpu.VMEM((row_count, feature_len), f32),
            dma((6,)),
            dma((4,)),
        ],
        ANY,
        mib=60,
    )(slot, lower[1], returned.reshape(slots, feature_len), lower[0])


def solution(mesh):
    placed = (
        P(("runs", "sec"), None),
        P(("runs", "sec"), None),
        P("runs", None),
        P(("runs", "sec")),
        P(("runs", "sec")),
    )
    return jax.shard_map(
        per_device, mesh=mesh, in_specs=placed, out_specs=P(("runs", "sec"), None), check_vma=False
    )
```
